32 devices in a mesh: sec: 4 (over y, core), blk: 2 (over x), gy: 4 (over z).
Axes of the slice: x: 2, y: 2, z: 4, core: 2. Of those that a mesh axis runs over, the one named last changes fastest.
Arguments:
- normalized_kelvin: float32 [32, 64, 512], P('blk', 'gy', 'sec'), may hold values from 0.6 to 2
- co2_molar_part: float32 [32, 64, 512], P('blk', 'gy', 'sec'), may hold values from 0.02 to 0.2
- h2o_molar_part: float32 [32, 64, 512], P('blk', 'gy', 'sec'), may hold values from 0.02 to 0.25
- particulate_scaled: float32 [32, 64, 512], P('blk', 'gy', 'sec'), may hold values from 0.01 to 1
- region_local_subgrids: int32 [4, 2, 4, 512], P('sec', 'blk', 'gy'), may hold values from 0 to 511, each once within a row
- entry_target_tile: int32 [64, 5], P(('sec', 'blk', 'gy')), may hold values from 0 to 63, as said below
- nonempty_entries_per_strip: int32 [64], P(('sec', 'blk', 'gy')), may hold values from 1 to 5, as said below
- transfer_matrix_tiles: bfloat16 [64, 5, 256, 256], P(('sec', 'blk', 'gy')), may hold values from -0.15625 to 0.15625
Outputs:
- temperature_new: float32 [32, 64, 512], P('blk', 'gy', 'sec')
- carbon_dioxide_new: float32 [32, 64, 512], P('blk', 'gy', 'sec')
- water_new: float32 [32, 64, 512], P('blk', 'gy', 'sec')
- soot_new: float32 [32, 64, 512], P('blk', 'gy', 'sec')
- source: float32 [32, 64, 512], P('blk', 'gy', 'sec')
The draws below stay inside these ranges and needn't reach their ends.
Inputs may be any that keep to these rules, and one draw needn't show every extreme that they name: `region_local_subgrids`: each device's row is a permutation of its 512 boxes. `entry_target_tile`: slot 0 of block row r names r itself; slots at or beyond the row's count are not read. `nonempty_entries_per_strip`: some block row has 5 live slots and some has 1.
All inputs are finite; a program needn't handle non-finite values.
Results may differ from the reference program's by a relative error of at most 0.0018.
Values may be sent and summed in bfloat16 or wider, within the bound.
A program may use at most 64 MiB of HBM per device.

```python
import math
import jax
import jax.numpy as jnp
from jax import lax

CX = 128
CY = 16
CZ = 16
BOX = 4
ZONE = 256
NNZ = 5
GRID_POINTS_EAST = 512
GRID_POINTS_NORTH = 64
GRID_POINTS_UP = 32
BOXES = 512
NBLOCKS = 64
N_SEC = 4
N_BLK = 2
N_GY = 4


def draw_entry_target_tile(key, part):
    local_key = jax.random.fold_in(key, 11)
    rows_index = jnp.arange(NBLOCKS, dtype=jnp.int32)[:, None]
    offsets = jax.random.randint(local_key, (NBLOCKS, NNZ), 1, NBLOCKS, dtype=jnp.int32)
    columns = (rows_index + offsets) % NBLOCKS
    return columns.at[:, 0].set(rows_index[:, 0]).astype(jnp.int32)


def draw_nonempty_entries_per_strip(key, part):
    local_key = jax.random.fold_in(key, 23)
    counts = jax.random.randint(local_key, (NBLOCKS,), 1, NNZ + 1, dtype=jnp.int32)
    return counts.at[0].set(NNZ).at[1].set(1).astype(jnp.int32)


def level_of(own_key, shape, split, smallest, high):
    factor_of, own = 1.0, jax.random.fold_in(own_key, 6)
    for dim, blocks in split:
        heights = jnp.exp(jax.random.uniform(jax.random.fold_in(own, dim), (blocks,), jnp.float32, smallest / len(split), high / len(split)))
        factor_of = factor_of * jnp.repeat(heights, shape[dim] // blocks).reshape([-1 if axis == dim else 1 for axis in range(len(shape))])
    return factor_of


def gaussian(stream_key, shape, width, reach, shards=(), held_as=jnp.bfloat16):
    result = width * jax.random.normal(stream_key, shape, jnp.float32)
    if shards:
        result = result * level_of(stream_key, shape, shards, -0.22, 0.18)
    return jnp.clip(result, -reach, reach).astype(held_as)


def setup_inputs(seed: int = 0) -> dict:
    key_of = jax.random.split(jax.random.key(seed), 9)
    return {
        "normalized_kelvin": jnp.clip(0.6 + 1.4 * jax.random.uniform(key_of[0], (GRID_POINTS_UP, GRID_POINTS_NORTH, GRID_POINTS_EAST), jnp.float32) ** level_of(key_of[0], (GRID_POINTS_UP, GRID_POINTS_NORTH, GRID_POINTS_EAST), ((0, 2), (1, 4), (2, 4)), -0.2, 0.2), 0.6, 2.0),
        "co2_molar_part": jnp.clip(0.02 + 0.18 * jax.random.uniform(key_of[1], (GRID_POINTS_UP, GRID_POINTS_NORTH, GRID_POINTS_EAST), jnp.float32) ** level_of(key_of[1], (GRID_POINTS_UP, GRID_POINTS_NORTH, GRID_POINTS_EAST), ((0, 2), (1, 4), (2, 4)), -0.2, 0.2), 0.02, 0.2),
        "h2o_molar_part": jnp.clip(0.02 + 0.23 * jax.random.uniform(key_of[2], (GRID_POINTS_UP, GRID_POINTS_NORTH, GRID_POINTS_EAST), jnp.float32) ** level_of(key_of[2], (GRID_POINTS_UP, GRID_POINTS_NORTH, GRID_POINTS_EAST), ((0, 2), (1, 4), (2, 4)), -0.2, 0.2), 0.02, 0.25),
        "particulate_scaled": jnp.clip(jnp.exp(math.log(1.0) - 4.6051702 * jax.random.uniform(key_of[3], (GRID_POINTS_UP, GRID_POINTS_NORTH, GRID_POINTS_EAST), jnp.float32) ** level_of(key_of[3], (GRID_POINTS_UP, GRID_POINTS_NORTH, GRID_POINTS_EAST), ((0, 2), (1, 4), (2, 4)), -0.2, 0.2)), 0.01, 1.0),
        "region_local_subgrids": jax.vmap(lambda own: jax.random.permutation(own, BOXES))(jax.random.split(key_of[4], N_SEC * N_BLK * N_GY)).reshape((N_SEC, N_BLK, N_GY, BOXES)).astype(jnp.int32),
        "entry_target_tile": draw_entry_target_tile(jax.random.fold_in(key_of[8], 71), 0),
        "nonempty_entries_per_strip": draw_nonempty_entries_per_strip(jax.random.fold_in(key_of[8], 71), 0),
        "transfer_matrix_tiles": gaussian(key_of[7], (NBLOCKS, NNZ, ZONE, ZONE), (ZONE * NNZ) ** -0.5, 0.15625, ((0, 32),)),
    }


diffusion_rates = (0.12, 0.1, 0.1, 0.02)
vapour_attenuation_rate = (0.4, 1.6, 6.4, 25.6)
mixture_share_offset = (0.3, 0.25, 0.2, 0.15)
mixture_share_slope = (-0.05, 0.02, 0.03, 0.01)
particulate_attenuation_rate = 1.5
radiance_multiplier = 0.05
heating_rate = 0.1


def radiant_output_of_region(normalized_kelvin, co2_molar_part, h2o_molar_part, particulate_scaled):
    molecular_constituents = co2_molar_part + h2o_molar_part
    overall_summation = jnp.zeros_like(normalized_kelvin)
    for region_position in range(4):
        greybody_share = mixture_share_offset[region_position] + mixture_share_slope[region_position] * normalized_kelvin
        overall_summation = overall_summation + greybody_share * (vapour_attenuation_rate[region_position] * molecular_constituents + particulate_attenuation_rate * particulate_scaled * normalized_kelvin)
    kelvin_tesseract = normalized_kelvin * normalized_kelvin * normalized_kelvin * normalized_kelvin
    return radiance_multiplier * kelvin_tesseract * overall_summation


def to_boxes(whole):
    shaped = whole.reshape(N_BLK, CZ // BOX, BOX, N_GY, CY // BOX, BOX, N_SEC, CX // BOX, BOX)
    summed = jnp.sum(shaped, axis=(2, 5, 8)) * (1.0 / (BOX * BOX * BOX))
    return summed.transpose(4, 0, 2, 1, 3, 5).reshape(N_SEC, N_BLK, N_GY, BOXES)


def from_boxes(parts):
    shaped = parts.reshape(N_SEC, N_BLK, N_GY, CZ // BOX, 1, CY // BOX, 1, CX // BOX, 1)
    spread = jnp.broadcast_to(shaped, (N_SEC, N_BLK, N_GY, CZ // BOX, BOX, CY // BOX, BOX, CX // BOX, BOX))
    spread = spread.reshape(N_SEC, N_BLK, N_GY, CZ, CY, CX)
    return spread.transpose(1, 3, 2, 4, 0, 5).reshape(GRID_POINTS_UP, GRID_POINTS_NORTH, GRID_POINTS_EAST)


def row_product(items):
    matrix, picked_row = items
    return jnp.einsum("kij,kj->i", matrix.astype(jnp.float32), picked_row.astype(jnp.float32))


def reference(normalized_kelvin, co2_molar_part, h2o_molar_part, particulate_scaled, region_local_subgrids, entry_target_tile, nonempty_entries_per_strip, transfer_matrix_tiles):
    constituent_arrays = jnp.stack([normalized_kelvin, co2_molar_part, h2o_molar_part, particulate_scaled])
    padded = jnp.pad(constituent_arrays, ((0, 0), (1, 1), (1, 1), (1, 1)))
    beside = padded[:, 2:, 1:-1, 1:-1] + padded[:, :-2, 1:-1, 1:-1]
    beside = beside + padded[:, 1:-1, 2:, 1:-1] + padded[:, 1:-1, :-2, 1:-1]
    beside = beside + padded[:, 1:-1, 1:-1, 2:] + padded[:, 1:-1, 1:-1, :-2]
    rates = jnp.array(diffusion_rates, jnp.float32)[:, None, None, None]
    swept = constituent_arrays + rates * (beside - 6.0 * constituent_arrays)
    radiated_energy_rate = radiant_output_of_region(normalized_kelvin, co2_molar_part, h2o_molar_part, particulate_scaled)
    box_parts = to_boxes(radiated_energy_rate)
    zone_emission = jnp.take_along_axis(box_parts, region_local_subgrids, axis=3)
    emitted = zone_emission.astype(jnp.bfloat16).reshape(NBLOCKS, ZONE)
    picked = emitted[entry_target_tile]
    live_slots = jnp.arange(NNZ, dtype=jnp.int32)[None, :] < nonempty_entries_per_strip[:, None]
    picked = jnp.where(live_slots[:, :, None], picked, jnp.zeros_like(picked))
    taken_in_light = lax.map(row_product, (transfer_matrix_tiles, picked))
    net_zone = taken_in_light.reshape(N_SEC, N_BLK, N_GY, BOXES) - zone_emission
    first = jnp.arange(N_SEC, dtype=jnp.int32)[:, None, None, None]
    second = jnp.arange(N_BLK, dtype=jnp.int32)[None, :, None, None]
    third = jnp.arange(N_GY, dtype=jnp.int32)[None, None, :, None]
    box_net = jnp.zeros_like(net_zone).at[first, second, third, region_local_subgrids].set(net_zone)
    source = from_boxes(box_net)
    return (swept[0] + heating_rate * source, swept[1], swept[2], swept[3], source)
```

```python
import functools

import jax
import jax.numpy as jnp
from jax import lax
from jax.experimental import pallas as pl
from jax.experimental.pallas import tpu as pltpu
from jax.sharding import PartitionSpec as P

BOX = 4
AXES = ("sec", "blk", "gy")

diffusion_rates = (0.12, 0.1, 0.1, 0.02)
vapour_attenuation_rate = (0.4, 1.6, 6.4, 25.6)
mixture_share_offset = (0.3, 0.25, 0.2, 0.15)
mixture_share_slope = (-0.05, 0.02, 0.03, 0.01)
particulate_attenuation_rate = 1.5
radiance_multiplier = 0.05
heating_rate = 0.1

SHARE_OFFSET = sum(mixture_share_offset)
SHARE_SLOPE = sum(mixture_share_slope)
VAPOUR_OFFSET = sum(b * k for b, k in zip(mixture_share_offset, vapour_attenuation_rate))
VAPOUR_SLOPE = sum(c * k for c, k in zip(mixture_share_slope, vapour_attenuation_rate))

MESH = pl.DeviceIdType.MESH
NT = (((1,), (1,)), ((), ()))
TN = (((0,), (0,)), ((), ()))


def iota(shape, dim):
    return lax.broadcasted_iota(jnp.int32, shape, dim)


def group_sum(value, axis):
    size = value.shape[axis]
    place = iota(value.shape, axis)
    for step in (1, 2):
        above = pltpu.roll(value, size - step, axis)
        below = pltpu.roll(value, step, axis)
        value = value + jnp.where((place & step) == 0, above, below)
    return value


def kernel(
    dims,
    counts,
    kelvin_hbm,
    co2_hbm,
    h2o_hbm,
    soot_hbm,
    order_hbm,
    tile_hbm,
    live_hbm,
    matrix_hbm,
    *rest,
):
    done, matrix, picked_out, mean_out, rows_out, spread_out = rest[:6]
    (
        fields,
        order_ref,
        gathered,
        z_out,
        y_out,
        x_out,
        z_in,
        y_in,
        x_in,
        tile_ref,
        live_ref,
        in_sem,
        face_send,
        face_recv,
        send_sem,
        recv_sem,
    ) = rest[6:]
    cz, cy, cx = dims
    n_sec, n_blk, n_gy = counts
    cells = cz * cy
    rows = matrix.shape[0]
    slots = matrix.shape[1]
    zones = order_ref.shape[1]
    zone = zones // rows
    n_plane = n_blk * n_gy
    sec, blk, gy = (lax.axis_index(a) for a in AXES)
    plane = blk * n_gy + gy
    me = sec * n_plane + plane
    n_all = n_sec * n_plane

    copies = [
        pltpu.make_async_copy(src, fields.at[i], in_sem.at[i])
        for i, src in enumerate((kelvin_hbm, co2_hbm, h2o_hbm, soot_hbm))
    ]
    copies.append(pltpu.make_async_copy(order_hbm, order_ref, in_sem.at[4]))
    copies.append(pltpu.make_async_copy(matrix_hbm, matrix, in_sem.at[5]))
    copies.append(pltpu.make_async_copy(tile_hbm, tile_ref, in_sem.at[6]))
    copies.append(pltpu.make_async_copy(live_hbm, live_ref, in_sem.at[7]))
    for copy in copies[:5] + copies[6:]:
        copy.start()

    def plane_peer(i):
        flat = lax.rem(me + i, n_all)
        return {
            "sec": lax.div(flat, n_plane),
            "blk": lax.rem(lax.div(flat, n_gy), n_blk),
            "gy": lax.rem(flat, n_gy),
        }

    def each(body):
        if n_all <= 32:
            for flat in range(n_all):

                @pl.when(me != flat)
                def _(flat=flat):
                    body(
                        {
                            "sec": flat // n_plane,
                            "blk": flat // n_gy % n_blk,
                            "gy": flat % n_gy,
                        }
                    )
        else:
            lax.fori_loop(1, n_all, lambda i, c: (body(plane_peer(i)), c)[1], 0)

    barrier = pltpu.get_barrier_semaphore()
    each(lambda peer: pl.semaphore_signal(barrier, inc=1, device_id=peer, device_id_type=MESH))

    places = (("sec", sec, n_sec), ("blk", blk, n_blk), ("gy", gy, n_gy))
    landing = (x_in, z_in, y_in)
    leaving = (x_out, z_out, y_out)
    for (_, at, size), land in zip(places, landing):
        for side, edge in ((0, 0), (1, size - 1)):

            @pl.when(at == edge)
            def _(land=land, side=side):
                land[side] = jnp.zeros(land.shape[1:], land.dtype)

    copies[4].wait()
    order = order_ref[...]
    across = cx // BOX
    x_shape = (cx, zones)
    r_shape = (cells // BOX, zones)
    x_at = iota(x_shape, 0)
    r_at = iota(r_shape, 0)
    same_x = lax.rem(order, across) == lax.div(x_at, BOX)
    box_row = lax.div(r_at, cy) * (cy // BOX) + lax.div(lax.rem(r_at, cy), BOX)
    same_r = lax.div(order, across) == box_row
    spread_x = jnp.where(same_x, 1.0, 0.0).astype(jnp.bfloat16)
    spread_out[...] = spread_x
    rows_out[...] = jnp.where(same_r, 1.0, 0.0)
    for copy in copies[:4]:
        copy.wait()
    copies[5].start()

    kelvin = fields[0]
    vapour = fields[1] + fields[2]
    soot_kelvin = fields[3] * kelvin
    share = vapour * (VAPOUR_OFFSET + VAPOUR_SLOPE * kelvin) + (
        particulate_attenuation_rate * soot_kelvin * (SHARE_OFFSET + SHARE_SLOPE * kelvin)
    )
    squared = kelvin * kelvin
    emission = radiance_multiplier * (squared * squared) * share
    slabs = emission.reshape(cz // BOX, BOX, cy, cx)
    slabs = (slabs[:, 0] + slabs[:, 1] + slabs[:, 2] + slabs[:, 3]).reshape(cells // BOX, cx)
    slabs = slabs * (1.0 / (BOX * BOX * BOX))
    upper = slabs.astype(jnp.bfloat16)
    lower = (slabs - upper.astype(jnp.float32)).astype(jnp.bfloat16)
    by_row = jnp.dot(
        jnp.concatenate([upper, lower], axis=0), spread_x, preferred_element_type=jnp.float32
    )
    by_row = by_row[: cells // BOX] + by_row[cells // BOX :]
    emitted = jnp.sum(jnp.where(same_r, by_row, 0.0), axis=0, keepdims=True)
    for r in range(rows):
        gathered[me * rows + r] = emitted[:, r * zone : (r + 1) * zone]

    lane = iota((cells, cx), 1)
    packed = jnp.zeros((cells, cx), jnp.float32)
    for f in range(4):
        field = fields.at[f]
        z_out[0, f] = field[pl.ds(0, cy), :]
        z_out[1, f] = field[pl.ds(cells - cy, cy), :]
        y_out[0, f] = field[pl.ds(0, cz, stride=cy), :]
        y_out[1, f] = field[pl.ds(cy - 1, cz, stride=cy), :]
        packed = jnp.where((lane >> 1) == f, pltpu.roll(field[...], 2 * f + 1, 1), packed)
    x_out[...] = jnp.transpose(packed)[:8]

    pl.semaphore_wait(barrier, n_all - 1)

    def push(start, length, peer, stage):
        block = gathered.at[pl.ds(start, length)]
        pltpu.make_async_remote_copy(
            src_ref=block,
            dst_ref=block,
            send_sem=send_sem.at[stage],
            recv_sem=recv_sem.at[stage],
            device_id=peer,
            device_id_type=MESH,
        ).start()

    def settle(length, sem):
        block = gathered.at[pl.ds(0, length)]
        pltpu.make_async_copy(block, block, sem).wait()

    each(lambda peer: push(me * rows, rows, peer, 0))

    def face(which, side):
        axis, at, _ = places[which]
        source = x_out if which == 0 else leaving[which].at[side]
        return pltpu.make_async_remote_copy(
            src_ref=source,
            dst_ref=landing[which].at[1 - side],
            send_sem=face_send.at[which, side],
            recv_sem=face_recv.at[which, 1 - side],
            device_id={axis: at + (2 * side - 1)},
            device_id_type=MESH,
        )

    def has(which, side):
        _, at, size = places[which]
        return at > 0 if side == 0 else at < size - 1

    for which in (1, 2, 0):
        for side in (0, 1):

            @pl.when(has(which, side))
            def _(which=which, side=side):
                face(which, side).start()

    mean_out[...] = group_sum(group_sum(slabs, 0), 1)
    place = iota((cells, cx), 0)
    y_place = lax.rem(place, cy)
    for f in range(4):
        value = fields[f]
        total = jnp.where(place >= cy, pltpu.roll(value, cy, 0), 0.0)
        total += jnp.where(place < cells - cy, pltpu.roll(value, cells - cy, 0), 0.0)
        total += jnp.where(y_place > 0, pltpu.roll(value, 1, 0), 0.0)
        total += jnp.where(y_place < cy - 1, pltpu.roll(value, cells - 1, 0), 0.0)
        total += jnp.where(lane > 0, pltpu.roll(value, 1, 1), 0.0)
        total += jnp.where(lane < cx - 1, pltpu.roll(value, cx - 1, 1), 0.0)
        done[f] = value + diffusion_rates[f] * (total - 6.0 * value)

    for which in (0, 1, 2):
        for side in (0, 1):

            @pl.when(has(which, side))
            def _(which=which, side=side):
                face(which, 1 - side).wait_recv()

    shape = (32, 4 * cx)
    row, column = iota(shape, 0) & 15, iota(shape, 1)
    chosen = ((row < 8) & (column == (row >> 1) * cx) & ((row & 1) == 0)) | (
        (row >= 8) & (column == ((row - 8) >> 1) * cx + cx - 1) & ((row & 1) == 1)
    )
    sides = jnp.concatenate([x_in[0], x_in[1]], axis=0)
    upper = sides.astype(jnp.bfloat16).astype(jnp.float32)
    x_add = lax.dot_general(
        jnp.concatenate([upper, sides - upper], axis=0),
        jnp.where(chosen, 1.0, 0.0),
        TN,
        preferred_element_type=jnp.float32,
    )
    for f in (1, 2, 3, 0):
        rate = diffusion_rates[f]
        out = done.at[f]
        out[...] += rate * x_add[:, f * cx : (f + 1) * cx]
        out[pl.ds(0, cy), :] += rate * z_in[0, f]
        out[pl.ds(cells - cy, cy), :] += rate * z_in[1, f]
        out[pl.ds(0, cz, stride=cy), :] += rate * y_in[0, f]
        out[pl.ds(cy - 1, cz, stride=cy), :] += rate * y_in[1, f]

    for copy in copies[5:]:
        copy.wait()
    settle((n_all - 1) * rows, recv_sem.at[0])

    for r in range(rows):
        for k in range(slots):
            tile = jnp.clip(tile_ref[r, k], 0, gathered.shape[0] - 1)
            picked_out[r, k] = jnp.where(k < live_ref[r], gathered[tile], 0.0)

    settle((n_all - 1) * rows, send_sem.at[0])
    for which in (0, 1, 2):
        for side in (0, 1):

            @pl.when(has(which, side))
            def _(which=which, side=side):
                face(which, side).wait_send()


def finish(dims, swept, matrix, picked, box_mean, same_r, spread_x, *rest):
    outs, heated, source_ref, sem = rest[:5], rest[5], rest[6], rest[7]
    cz, cy, cx = dims
    cells = cz * cy
    rows, slots, zone, _ = matrix.shape
    copies = [
        pltpu.make_async_copy(source, out, sem.at[i])
        for i, (source, out) in enumerate(
            zip((heated, swept.at[1], swept.at[2], swept.at[3], source_ref), outs)
        )
    ]
    for copy in copies[1:4]:
        copy.start()

    absorbed = []
    for r in range(rows):
        total = jnp.zeros((1, zone), jnp.float32)
        for k in range(slots):
            total += lax.dot_general(
                picked[r, k].astype(jnp.bfloat16),
                matrix[r, k],
                NT,
                preferred_element_type=jnp.float32,
            )
        absorbed.append(total)
    absorbed = jnp.concatenate(absorbed, axis=1)
    high = absorbed.astype(jnp.bfloat16).astype(jnp.float32)
    low = absorbed - high
    mask = same_r[...]
    both = jnp.concatenate([mask * high, mask * low], axis=0).astype(jnp.bfloat16)
    carried = lax.dot_general(both, spread_x[...], NT, preferred_element_type=jnp.float32)
    net = carried[: cells // BOX] + carried[cells // BOX :] - box_mean[...]
    source = jnp.broadcast_to(
        net.reshape(cz // BOX, 1, cy, cx), (cz // BOX, BOX, cy, cx)
    ).reshape(cells, cx)
    source_ref[...] = source
    copies[4].start()
    heated[...] = swept[0] + heating_rate * source
    copies[0].start()
    for copy in copies:
        copy.wait()


def solution(mesh):
    counts = tuple(mesh.shape[a] for a in AXES)

    def local(kelvin, co2, h2o, soot, order, tiles, live, matrix):
        dims = kelvin.shape
        cz, cy, cx = dims
        cells = cz * cy
        rows = matrix.shape[0]
        zone = matrix.shape[2]
        blocks = counts[0] * counts[1] * counts[2] * rows
        flat = [a.reshape(cells, cx) for a in (kelvin, co2, h2o, soot)]
        order = order.reshape(1, -1)
        anywhere = pl.BlockSpec(memory_space=pl.ANY)
        f32 = jnp.float32
        vmem = pl.BlockSpec(memory_space=pltpu.VMEM)
        zones = order.shape[1]
        slots = matrix.shape[1]
        parts = pl.pallas_call(
            functools.partial(kernel, dims, counts),
            out_shape=[
                pltpu.VMEM((4, cells, cx), f32),
                pltpu.VMEM(matrix.shape, matrix.dtype),
                pltpu.VMEM((rows, slots, 1, zone), f32),
                pltpu.VMEM((cells // BOX, cx), f32),
                pltpu.VMEM((cells // BOX, zones), f32),
                pltpu.VMEM((cx, zones), jnp.bfloat16),
            ],
            in_specs=[anywhere] * 8,
            out_specs=[vmem] * 6,
            scratch_shapes=[
                pltpu.VMEM((4, cells, cx), f32),
                pltpu.VMEM(order.shape, jnp.int32),
                pltpu.VMEM((blocks, 1, zone), f32),
                pltpu.VMEM((2, 4, cy, cx), f32),
                pltpu.VMEM((2, 4, cz, cx), f32),
                pltpu.VMEM((8, cells), f32),
                pltpu.VMEM((2, 4, cy, cx), f32),
                pltpu.VMEM((2, 4, cz, cx), f32),
                pltpu.VMEM((2, 8, cells), f32),
                pltpu.SMEM(tiles.shape, tiles.dtype),
                pltpu.SMEM(live.shape, live.dtype),
                pltpu.SemaphoreType.DMA((8,)),
                pltpu.SemaphoreType.DMA((3, 2)),
                pltpu.SemaphoreType.DMA((3, 2)),
                pltpu.SemaphoreType.DMA((2,)),
                pltpu.SemaphoreType.DMA((2,)),
            ],
            compiler_params=pltpu.CompilerParams(collective_id=0, has_side_effects=True),
        )(*flat, order, tiles, live, matrix)
        outs = pl.pallas_call(
            functools.partial(finish, dims),
            out_shape=[jax.ShapeDtypeStruct((cells, cx), f32)] * 5,
            in_specs=[vmem] * 6,
            out_specs=[anywhere] * 5,
            scratch_shapes=[
                pltpu.VMEM((cells, cx), f32),
                pltpu.VMEM((cells, cx), f32),
                pltpu.SemaphoreType.DMA((5,)),
            ],
            compiler_params=pltpu.CompilerParams(vmem_limit_bytes=16 << 20),
        )(*parts)
        return tuple(o.reshape(dims) for o in outs)

    cell = P("blk", "gy", "sec")
    block = P(AXES)
    return jax.shard_map(
        local,
        mesh=mesh,
        in_specs=(cell,) * 4 + (P("sec", "blk", "gy", None), P(AXES, None), block, P(AXES, None, None, None)),
        out_specs=(cell,) * 5,
        check_vma=False,
    )
```

```python
import functools

import jax
import jax.numpy as jnp
from jax import lax
from jax.experimental import pallas as pl
from jax.experimental.pallas import tpu as pltpu
from jax.sharding import PartitionSpec as P

BOX = 4
AXES = ("sec", "blk", "gy")

diffusion_rates = (0.12, 0.1, 0.1, 0.02)
vapour_attenuation_rate = (0.4, 1.6, 6.4, 25.6)
mixture_share_offset = (0.3, 0.25, 0.2, 0.15)
mixture_share_slope = (-0.05, 0.02, 0.03, 0.01)
particulate_attenuation_rate = 1.5
radiance_multiplier = 0.05
heating_rate = 0.1

SHARE_OFFSET = sum(mixture_share_offset)
SHARE_SLOPE = sum(mixture_share_slope)
VAPOUR_OFFSET = sum(b * k for b, k in zip(mixture_share_offset, vapour_attenuation_rate))
VAPOUR_SLOPE = sum(c * k for c, k in zip(mixture_share_slope, vapour_attenuation_rate))

MESH = pl.DeviceIdType.MESH
NT = (((1,), (1,)), ((), ()))
TN = (((0,), (0,)), ((), ()))


def iota(shape, dim):
    return lax.broadcasted_iota(jnp.int32, shape, dim)


def group_sum(value, axis):
    size = value.shape[axis]
    place = iota(value.shape, axis)
    for step in (1, 2):
        above = pltpu.roll(value, size - step, axis)
        below = pltpu.roll(value, step, axis)
        value = value + jnp.where((place & step) == 0, above, below)
    return value


def kernel(
    dims,
    counts,
    kelvin_hbm,
    co2_hbm,
    h2o_hbm,
    soot_hbm,
    order_hbm,
    tile_hbm,
    live_hbm,
    matrix_hbm,
    *rest,
):
    done, matrix, picked_out, mean_out, rows_out, spread_out = rest[:6]
    (
        fields,
        order_ref,
        gathered,
        z_out,
        y_out,
        x_out,
        z_in,
        y_in,
        x_in,
        tile_ref,
        live_ref,
        in_sem,
        face_send,
        face_recv,
        send_sem,
        recv_sem,
        far_sem,
    ) = rest[6:]
    cz, cy, cx = dims
    n_sec, n_blk, n_gy = counts
    cells = cz * cy
    rows = matrix.shape[0]
    slots = matrix.shape[1]
    zones = order_ref.shape[1]
    zone = zones // rows
    n_plane = n_blk * n_gy
    sec, blk, gy = (lax.axis_index(a) for a in AXES)
    plane = blk * n_gy + gy
    me = sec * n_plane + plane
    n_all = n_sec * n_plane

    copies = [
        pltpu.make_async_copy(src, fields.at[i], in_sem.at[i])
        for i, src in enumerate((kelvin_hbm, co2_hbm, h2o_hbm, soot_hbm))
    ]
    copies.append(pltpu.make_async_copy(order_hbm, order_ref, in_sem.at[4]))
    copies.append(pltpu.make_async_copy(matrix_hbm, matrix, in_sem.at[5]))
    copies.append(pltpu.make_async_copy(tile_hbm, tile_ref, in_sem.at[6]))
    copies.append(pltpu.make_async_copy(live_hbm, live_ref, in_sem.at[7]))
    for copy in copies[:5] + copies[6:]:
        copy.start()

    level = n_sec * n_blk

    def steps(sec, blk, gy):
        return sec // 2 + blk + gy

    def beside(peer):
        away = [abs(peer[a] - at) for a, at in zip(AXES, (sec, blk, gy))]
        return away[0] + away[1] + away[2] == 1

    def each(chosen, body):
        if n_all <= 32:
            for r in range(n_all):
                peer = {"sec": r % n_sec, "blk": r // n_sec % n_blk, "gy": r // level}

                @pl.when(chosen(peer))
                def _(peer=peer):
                    body(peer)
        else:

            @pl.loop(0, n_all)
            def _(r):
                peer = {
                    "sec": lax.rem(r, n_sec),
                    "blk": lax.rem(lax.div(r, n_sec), n_blk),
                    "gy": lax.div(r, level),
                }

                @pl.when(chosen(peer))
                def _():
                    body(peer)

    def other(peer):
        return (peer["sec"] * n_blk + peer["blk"]) * n_gy + peer["gy"] != me

    def first(peer):
        return jnp.asarray(steps(**peer) <= 1)

    mine = steps(sec, blk, gy)
    early = mine <= 1
    last = mine == (n_sec - 1) // 2 + n_blk + n_gy - 2
    n_first = sum(
        a // 2 + b + c <= 1 for a in range(n_sec) for b in range(n_blk) for c in range(n_gy)
    )

    def both(a, b):
        return jnp.logical_and(a, b)

    def either(a, b):
        return jnp.logical_or(a, b)

    def greeted(peer):
        return both(other(peer), either(early, either(~first(peer), beside(peer))))

    def greet(sem):
        return lambda peer: pl.semaphore_signal(
            sem, inc=1, device_id=peer, device_id_type=MESH
        )

    barrier = pltpu.get_barrier_semaphore()
    each(greeted, greet(barrier))

    places = (("sec", sec, n_sec), ("blk", blk, n_blk), ("gy", gy, n_gy))
    late = jnp.int32(0)
    for axis, at, size in places:
        for move, inside in ((-1, at > 0), (1, at < size - 1)):
            there = dict(zip(AXES, (sec, blk, gy)))
            there[axis] = at + move
            late += both(inside, steps(**there) > 1).astype(jnp.int32)

    def enter():
        pl.semaphore_wait(barrier, jnp.where(early, n_first - 1 + late, n_all - 1))
        each(
            lambda peer: both(first(peer), both(~early, ~beside(peer))),
            greet(far_sem),
        )

    @pl.when(last)
    def _():
        enter()

    landing = (x_in, z_in, y_in)
    leaving = (x_out, z_out, y_out)
    for (_, at, size), land in zip(places, landing):
        for side, edge in ((0, 0), (1, size - 1)):

            @pl.when(at == edge)
            def _(land=land, side=side):
                land[side] = jnp.zeros(land.shape[1:], land.dtype)

    copies[4].wait()
    order = order_ref[...]
    across = cx // BOX
    x_shape = (cx, zones)
    r_shape = (cells // BOX, zones)
    x_at = iota(x_shape, 0)
    r_at = iota(r_shape, 0)
    same_x = lax.rem(order, across) == lax.div(x_at, BOX)
    box_row = lax.div(r_at, cy) * (cy // BOX) + lax.div(lax.rem(r_at, cy), BOX)
    same_r = lax.div(order, across) == box_row
    spread_x = jnp.where(same_x, 1.0, 0.0).astype(jnp.bfloat16)
    spread_out[...] = spread_x
    rows_out[...] = jnp.where(same_r, 1.0, 0.0)
    for copy in copies[:4]:
        copy.wait()
    copies[5].start()

    kelvin = fields[0]
    vapour = fields[1] + fields[2]
    soot_kelvin = fields[3] * kelvin
    share = vapour * (VAPOUR_OFFSET + VAPOUR_SLOPE * kelvin) + (
        particulate_attenuation_rate * soot_kelvin * (SHARE_OFFSET + SHARE_SLOPE * kelvin)
    )
    squared = kelvin * kelvin
    emission = radiance_multiplier * (squared * squared) * share
    slabs = emission.reshape(cz // BOX, BOX, cy, cx)
    slabs = (slabs[:, 0] + slabs[:, 1] + slabs[:, 2] + slabs[:, 3]).reshape(cells // BOX, cx)
    slabs = slabs * (1.0 / (BOX * BOX * BOX))
    upper = slabs.astype(jnp.bfloat16)
    lower = (slabs - upper.astype(jnp.float32)).astype(jnp.bfloat16)
    by_row = jnp.dot(
        jnp.concatenate([upper, lower], axis=0), spread_x, preferred_element_type=jnp.float32
    )
    by_row = by_row[: cells // BOX] + by_row[cells // BOX :]
    emitted = jnp.sum(jnp.where(same_r, by_row, 0.0), axis=0, keepdims=True)
    for r in range(rows):
        gathered[me * rows + r] = emitted[:, r * zone : (r + 1) * zone]

    def push(start, length, peer, stage):
        block = gathered.at[pl.ds(start, length)]
        pltpu.make_async_remote_copy(
            src_ref=block,
            dst_ref=block,
            send_sem=send_sem.at[stage],
            recv_sem=recv_sem.at[stage],
            device_id=peer,
            device_id_type=MESH,
        ).start()

    def settle(length, sem):
        block = gathered.at[pl.ds(0, length)]
        pltpu.make_async_copy(block, block, sem).wait()

    @pl.when(~last)
    def _():
        enter()

    each(
        lambda peer: both(other(peer), either(~early, first(peer))),
        lambda peer: push(me * rows, rows, peer, 0),
    )

    lane = iota((cells, cx), 1)
    packed = jnp.zeros((cells, cx), jnp.float32)
    for f in range(4):
        field = fields.at[f]
        z_out[0, f] = field[pl.ds(0, cy), :]
        z_out[1, f] = field[pl.ds(cells - cy, cy), :]
        y_out[0, f] = field[pl.ds(0, cz, stride=cy), :]
        y_out[1, f] = field[pl.ds(cy - 1, cz, stride=cy), :]
        packed = jnp.where((lane >> 1) == f, pltpu.roll(field[...], 2 * f + 1, 1), packed)
    x_out[...] = jnp.transpose(packed)[:8]

    def face(which, side):
        axis, at, _ = places[which]
        source = x_out if which == 0 else leaving[which].at[side]
        return pltpu.make_async_remote_copy(
            src_ref=source,
            dst_ref=landing[which].at[1 - side],
            send_sem=face_send.at[which, side],
            recv_sem=face_recv.at[which, 1 - side],
            device_id={axis: at + (2 * side - 1)},
            device_id_type=MESH,
        )

    def has(which, side):
        _, at, size = places[which]
        return at > 0 if side == 0 else at < size - 1

    def launch(side):
        for which in (1, 2, 0):

            @pl.when(has(which, side))
            def _(which=which):
                face(which, side).start()

    launch(0)
    launch(1)

    mean_out[...] = group_sum(group_sum(slabs, 0), 1)
    place = iota((cells, cx), 0)
    y_place = lax.rem(place, cy)
    for f in range(4):
        value = fields[f]
        total = jnp.where(place >= cy, pltpu.roll(value, cy, 0), 0.0)
        total += jnp.where(place < cells - cy, pltpu.roll(value, cells - cy, 0), 0.0)
        total += jnp.where(y_place > 0, pltpu.roll(value, 1, 0), 0.0)
        total += jnp.where(y_place < cy - 1, pltpu.roll(value, cells - 1, 0), 0.0)
        total += jnp.where(lane > 0, pltpu.roll(value, 1, 1), 0.0)
        total += jnp.where(lane < cx - 1, pltpu.roll(value, cx - 1, 1), 0.0)
        done[f] = value + diffusion_rates[f] * (total - 6.0 * value)

    @pl.when(early)
    def _():
        pl.semaphore_wait(far_sem, n_all - n_first - late)
        each(lambda peer: ~first(peer), lambda peer: push(me * rows, rows, peer, 0))

    for which in (0, 1, 2):
        for side in (0, 1):

            @pl.when(has(which, side))
            def _(which=which, side=side):
                face(which, 1 - side).wait_recv()

    shape = (32, 4 * cx)
    row, column = iota(shape, 0) & 15, iota(shape, 1)
    chosen = ((row < 8) & (column == (row >> 1) * cx) & ((row & 1) == 0)) | (
        (row >= 8) & (column == ((row - 8) >> 1) * cx + cx - 1) & ((row & 1) == 1)
    )
    sides = jnp.concatenate([x_in[0], x_in[1]], axis=0)
    upper = sides.astype(jnp.bfloat16).astype(jnp.float32)
    x_add = lax.dot_general(
        jnp.concatenate([upper, sides - upper], axis=0),
        jnp.where(chosen, 1.0, 0.0),
        TN,
        preferred_element_type=jnp.float32,
    )
    for f in (1, 2, 3, 0):
        rate = diffusion_rates[f]
        out = done.at[f]
        out[...] += rate * x_add[:, f * cx : (f + 1) * cx]
        out[pl.ds(0, cy), :] += rate * z_in[0, f]
        out[pl.ds(cells - cy, cy), :] += rate * z_in[1, f]
        out[pl.ds(0, cz, stride=cy), :] += rate * y_in[0, f]
        out[pl.ds(cy - 1, cz, stride=cy), :] += rate * y_in[1, f]

    for copy in copies[5:]:
        copy.wait()
    settle((n_all - 1) * rows, recv_sem.at[0])

    for r in range(rows):
        for k in range(slots):
            tile = jnp.clip(tile_ref[r, k], 0, gathered.shape[0] - 1)
            picked_out[r, k] = jnp.where(k < live_ref[r], gathered[tile], 0.0)

    settle((n_all - 1) * rows, send_sem.at[0])
    for which in (0, 1, 2):
        for side in (0, 1):

            @pl.when(has(which, side))
            def _(which=which, side=side):
                face(which, side).wait_send()


def finish(dims, swept, matrix, picked, box_mean, same_r, spread_x, *rest):
    outs, heated, source_ref, sem = rest[:5], rest[5], rest[6], rest[7]
    cz, cy, cx = dims
    cells = cz * cy
    rows, slots, zone, _ = matrix.shape
    copies = [
        pltpu.make_async_copy(source, out, sem.at[i])
        for i, (source, out) in enumerate(
            zip((heated, swept.at[1], swept.at[2], swept.at[3], source_ref), outs)
        )
    ]
    for copy in copies[1:4]:
        copy.start()

    absorbed = []
    for r in range(rows):
        total = jnp.zeros((1, zone), jnp.float32)
        for k in range(slots):
            total += lax.dot_general(
                picked[r, k].astype(jnp.bfloat16),
                matrix[r, k],
                NT,
                preferred_element_type=jnp.float32,
            )
        absorbed.append(total)
    absorbed = jnp.concatenate(absorbed, axis=1)
    high = absorbed.astype(jnp.bfloat16).astype(jnp.float32)
    low = absorbed - high
    mask = same_r[...]
    both = jnp.concatenate([mask * high, mask * low], axis=0).astype(jnp.bfloat16)
    carried = lax.dot_general(both, spread_x[...], NT, preferred_element_type=jnp.float32)
    net = carried[: cells // BOX] + carried[cells // BOX :] - box_mean[...]
    source = jnp.broadcast_to(
        net.reshape(cz // BOX, 1, cy, cx), (cz // BOX, BOX, cy, cx)
    ).reshape(cells, cx)
    source_ref[...] = source
    copies[4].start()
    heated[...] = swept[0] + heating_rate * source
    copies[0].start()
    for copy in copies:
        copy.wait()


def solution(mesh):
    counts = tuple(mesh.shape[a] for a in AXES)

    def local(kelvin, co2, h2o, soot, order, tiles, live, matrix):
        dims = kelvin.shape
        cz, cy, cx = dims
        cells = cz * cy
        rows = matrix.shape[0]
        zone = matrix.shape[2]
        blocks = counts[0] * counts[1] * counts[2] * rows
        flat = [a.reshape(cells, cx) for a in (kelvin, co2, h2o, soot)]
        order = order.reshape(1, -1)
        anywhere = pl.BlockSpec(memory_space=pl.ANY)
        f32 = jnp.float32
        vmem = pl.BlockSpec(memory_space=pltpu.VMEM)
        zones = order.shape[1]
        slots = matrix.shape[1]
        parts = pl.pallas_call(
            functools.partial(kernel, dims, counts),
            out_shape=[
                pltpu.VMEM((4, cells, cx), f32),
                pltpu.VMEM(matrix.shape, matrix.dtype),
                pltpu.VMEM((rows, slots, 1, zone), f32),
                pltpu.VMEM((cells // BOX, cx), f32),
                pltpu.VMEM((cells // BOX, zones), f32),
                pltpu.VMEM((cx, zones), jnp.bfloat16),
            ],
            in_specs=[anywhere] * 8,
            out_specs=[vmem] * 6,
            scratch_shapes=[
                pltpu.VMEM((4, cells, cx), f32),
                pltpu.VMEM(order.shape, jnp.int32),
                pltpu.VMEM((blocks, 1, zone), f32),
                pltpu.VMEM((2, 4, cy, cx), f32),
                pltpu.VMEM((2, 4, cz, cx), f32),
                pltpu.VMEM((8, cells), f32),
                pltpu.VMEM((2, 4, cy, cx), f32),
                pltpu.VMEM((2, 4, cz, cx), f32),
                pltpu.VMEM((2, 8, cells), f32),
                pltpu.SMEM(tiles.shape, tiles.dtype),
                pltpu.SMEM(live.shape, live.dtype),
                pltpu.SemaphoreType.DMA((8,)),
                pltpu.SemaphoreType.DMA((3, 2)),
                pltpu.SemaphoreType.DMA((3, 2)),
                pltpu.SemaphoreType.DMA((1,)),
                pltpu.SemaphoreType.DMA((1,)),
                pltpu.SemaphoreType.REGULAR,
            ],
            compiler_params=pltpu.CompilerParams(collective_id=0, has_side_effects=True),
        )(*flat, order, tiles, live, matrix)
        outs = pl.pallas_call(
            functools.partial(finish, dims),
            out_shape=[jax.ShapeDtypeStruct((cells, cx), f32)] * 5,
            in_specs=[vmem] * 6,
            out_specs=[anywhere] * 5,
            scratch_shapes=[
                pltpu.VMEM((cells, cx), f32),
                pltpu.VMEM((cells, cx), f32),
                pltpu.SemaphoreType.DMA((5,)),
            ],
            compiler_params=pltpu.CompilerParams(vmem_limit_bytes=16 << 20),
        )(*parts)
        return tuple(o.reshape(dims) for o in outs)

    cell = P("blk", "gy", "sec")
    block = P(AXES)
    return jax.shard_map(
        local,
        mesh=mesh,
        in_specs=(cell,) * 4 + (P("sec", "blk", "gy", None), P(AXES, None), block, P(AXES, None, None, None)),
        out_specs=(cell,) * 5,
        check_vma=False,
    )
```

```python
import functools

import jax
import jax.numpy as jnp
from jax import lax
from jax.experimental import pallas as pl
from jax.experimental.pallas import tpu as pltpu
from jax.sharding import PartitionSpec as P

BOX = 4
AXES = ("sec", "blk", "gy")

diffusion_rates = (0.12, 0.1, 0.1, 0.02)
vapour_attenuation_rate = (0.4, 1.6, 6.4, 25.6)
mixture_share_offset = (0.3, 0.25, 0.2, 0.15)
mixture_share_slope = (-0.05, 0.02, 0.03, 0.01)
particulate_attenuation_rate = 1.5
radiance_multiplier = 0.05
heating_rate = 0.1

SHARE_OFFSET = sum(mixture_share_offset)
SHARE_SLOPE = sum(mixture_share_slope)
VAPOUR_OFFSET = sum(b * k for b, k in zip(mixture_share_offset, vapour_attenuation_rate))
VAPOUR_SLOPE = sum(c * k for c, k in zip(mixture_share_slope, vapour_attenuation_rate))

MESH = pl.DeviceIdType.MESH
NN = (((1,), (0,)), ((), ()))
TN = (((0,), (0,)), ((), ()))


def iota(shape, dim):
    return lax.broadcasted_iota(jnp.int32, shape, dim)


def group_sum(value, axis):
    size = value.shape[axis]
    place = iota(value.shape, axis)
    for step in (1, 2):
        above = pltpu.roll(value, size - step, axis)
        below = pltpu.roll(value, step, axis)
        value = value + jnp.where((place & step) == 0, above, below)
    return value


def kernel(
    dims,
    counts,
    kelvin_hbm,
    co2_hbm,
    h2o_hbm,
    soot_hbm,
    order_hbm,
    tile_hbm,
    live_hbm,
    matrix_hbm,
    *rest,
):
    done, flipped, picked_out, mean_out, rows_out, spread_out = rest[:6]
    (
        fields,
        order_ref,
        matrix,
        gathered,
        z_out,
        y_out,
        x_out,
        z_in,
        y_in,
        x_in,
        tile_ref,
        live_ref,
        field_sem,
        small_sem,
        face_send,
        face_recv,
        send_sem,
        recv_sem,
        far_sem,
    ) = rest[6:]
    cz, cy, cx = dims
    n_sec, n_blk, n_gy = counts
    cells = cz * cy
    rows = matrix.shape[0]
    slots = matrix.shape[1]
    zones = order_ref.shape[1]
    zone = zones // rows
    n_plane = n_blk * n_gy
    sec, blk, gy = (lax.axis_index(a) for a in AXES)
    plane = blk * n_gy + gy
    me = sec * n_plane + plane
    n_all = n_sec * n_plane

    n_slab = cz // BOX
    slab = BOX * cy
    pltpu.make_async_copy(order_hbm, order_ref, small_sem.at[0]).start()
    for t in range(n_slab):
        part = pl.ds(t * slab, slab)
        for i, src in enumerate((kelvin_hbm, co2_hbm, h2o_hbm, soot_hbm)):
            pltpu.make_async_copy(src.at[part], fields.at[i, part], field_sem.at[0]).start()

    def settle(ref, sem):
        pltpu.make_async_copy(ref, ref, sem).wait()

    level = n_sec * n_blk

    def steps(sec, blk, gy):
        return sec // 2 + blk + gy

    def beside(peer):
        away = [abs(peer[a] - at) for a, at in zip(AXES, (sec, blk, gy))]
        return away[0] + away[1] + away[2] == 1

    def each(chosen, body):
        if n_all <= 32:
            for r in range(n_all):
                peer = {"sec": r % n_sec, "blk": r // n_sec % n_blk, "gy": r // level}

                @pl.when(chosen(peer))
                def _(peer=peer):
                    body(peer)
        else:

            @pl.loop(0, n_all)
            def _(r):
                peer = {
                    "sec": lax.rem(r, n_sec),
                    "blk": lax.rem(lax.div(r, n_sec), n_blk),
                    "gy": lax.div(r, level),
                }

                @pl.when(chosen(peer))
                def _():
                    body(peer)

    def other(peer):
        return (peer["sec"] * n_blk + peer["blk"]) * n_gy + peer["gy"] != me

    def first(peer):
        return jnp.asarray(steps(**peer) <= 1)

    mine = steps(sec, blk, gy)
    early = mine <= 1
    last = mine == (n_sec - 1) // 2 + n_blk + n_gy - 2
    n_first = sum(
        a // 2 + b + c <= 1 for a in range(n_sec) for b in range(n_blk) for c in range(n_gy)
    )

    def both(a, b):
        return jnp.logical_and(a, b)

    def either(a, b):
        return jnp.logical_or(a, b)

    def greeted(peer):
        return both(other(peer), either(early, either(~first(peer), beside(peer))))

    def greet(sem):
        return lambda peer: pl.semaphore_signal(
            sem, inc=1, device_id=peer, device_id_type=MESH
        )

    barrier = pltpu.get_barrier_semaphore()
    each(greeted, greet(barrier))

    places = (("sec", sec, n_sec), ("blk", blk, n_blk), ("gy", gy, n_gy))
    late = jnp.int32(0)
    for axis, at, size in places:
        for move, inside in ((-1, at > 0), (1, at < size - 1)):
            there = dict(zip(AXES, (sec, blk, gy)))
            there[axis] = at + move
            late += both(inside, steps(**there) > 1).astype(jnp.int32)

    def enter():
        pl.semaphore_wait(barrier, jnp.where(early, n_first - 1 + late, n_all - 1))
        each(
            lambda peer: both(first(peer), both(~early, ~beside(peer))),
            greet(far_sem),
        )

    @pl.when(last)
    def _():
        enter()

    landing = (x_in, z_in, y_in)
    leaving = (x_out, z_out, y_out)
    for (_, at, size), land in zip(places, landing):
        for side, edge in ((0, 0), (1, size - 1)):

            @pl.when(at == edge)
            def _(land=land, side=side):
                land[side] = jnp.zeros(land.shape[1:], land.dtype)

    settle(order_ref, small_sem.at[0])
    order = order_ref[...]
    tile_copy = pltpu.make_async_copy(tile_hbm, tile_ref, small_sem.at[0])
    tile_copy.start()
    across = cx // BOX
    x_shape = (cx, zones)
    r_shape = (cells // BOX, zones)
    x_at = iota(x_shape, 0)
    r_at = iota(r_shape, 0)
    same_x = lax.rem(order, across) == lax.div(x_at, BOX)
    box_row = lax.div(r_at, cy) * (cy // BOX) + lax.div(lax.rem(r_at, cy), BOX)
    same_r = lax.div(order, across) == box_row
    spread_x = jnp.where(same_x, 1.0, 0.0).astype(jnp.bfloat16)
    rows_out[...] = jnp.where(same_r, 1.0, 0.0)
    total = jnp.zeros((cy, zones), jnp.float32)
    means = []
    settle(fields, field_sem.at[0])
    matrix_copy = pltpu.make_async_copy(matrix_hbm, matrix, field_sem.at[0])
    matrix_copy.start()
    halves = []
    for t in range(n_slab):
        kelvin, co2, h2o, soot = (fields[i, pl.ds(t * slab, slab), :] for i in range(4))
        vapour = co2 + h2o
        soot_kelvin = soot * kelvin
        share = vapour * (VAPOUR_OFFSET + VAPOUR_SLOPE * kelvin) + (
            particulate_attenuation_rate * soot_kelvin * (SHARE_OFFSET + SHARE_SLOPE * kelvin)
        )
        squared = kelvin * kelvin
        emission = (radiance_multiplier / BOX**3) * (squared * squared) * share
        emission = emission.reshape(BOX, cy, cx)
        mean = emission[0] + emission[1] + emission[2] + emission[3]
        means.append(mean)
        upper = mean.astype(jnp.bfloat16).astype(jnp.float32)
        halves += [upper, mean - upper]
    by_row = jnp.dot(
        jnp.concatenate(halves, axis=0).astype(jnp.bfloat16),
        spread_x,
        preferred_element_type=jnp.float32,
    )
    for t in range(n_slab):
        part = by_row[2 * t * cy : (2 * t + 1) * cy] + by_row[(2 * t + 1) * cy : (2 * t + 2) * cy]
        total += jnp.where(same_r[t * cy : (t + 1) * cy], part, 0.0)
    slabs = jnp.concatenate(means, axis=0)
    emitted = jnp.sum(total, axis=0, keepdims=True)
    for r in range(rows):
        gathered[me * rows + r] = emitted[:, r * zone : (r + 1) * zone]

    def push(start, length, peer, stage):
        block = gathered.at[pl.ds(start, length)]
        pltpu.make_async_remote_copy(
            src_ref=block,
            dst_ref=block,
            send_sem=send_sem.at[stage],
            recv_sem=recv_sem.at[stage],
            device_id=peer,
            device_id_type=MESH,
        ).start()

    @pl.when(~last)
    def _():
        enter()

    each(
        lambda peer: both(other(peer), either(~early, first(peer))),
        lambda peer: push(me * rows, rows, peer, 0),
    )

    lane = iota((cells, cx), 1)
    packed = jnp.zeros((cells, cx), jnp.float32)
    for f in range(4):
        field = fields.at[f]
        z_out[0, f] = field[pl.ds(0, cy), :]
        z_out[1, f] = field[pl.ds(cells - cy, cy), :]
        y_out[0, f] = field[pl.ds(0, cz, stride=cy), :]
        y_out[1, f] = field[pl.ds(cy - 1, cz, stride=cy), :]
        packed = jnp.where((lane >> 1) == f, pltpu.roll(field[...], 2 * f + 1, 1), packed)
    x_out[...] = jnp.transpose(packed)[:8]

    def face(which, side):
        axis, at, _ = places[which]
        source = x_out if which == 0 else leaving[which].at[side]
        return pltpu.make_async_remote_copy(
            src_ref=source,
            dst_ref=landing[which].at[1 - side],
            send_sem=face_send.at[which],
            recv_sem=face_recv.at[which],
            device_id={axis: at + (2 * side - 1)},
            device_id_type=MESH,
        )

    def has(which, side):
        _, at, size = places[which]
        return at > 0 if side == 0 else at < size - 1

    def finish_faces(sem):
        for which in (0, 1, 2):
            low, high = has(which, 0), has(which, 1)
            land = landing[which]

            @pl.when(both(low, high))
            def _(which=which, land=land):
                settle(land, sem.at[which])

            @pl.when(low != high)
            def _(which=which, land=land):
                settle(land.at[0], sem.at[which])

    def launch(side):
        for which in (1, 2, 0):

            @pl.when(has(which, side))
            def _(which=which):
                face(which, side).start()

    launch(0)
    launch(1)

    mean_out[...] = group_sum(group_sum(slabs, 0), 1)
    place = iota((cells, cx), 0)
    y_place = lax.rem(place, cy)
    for f in range(4):
        value = fields[f]
        total = jnp.where(place >= cy, pltpu.roll(value, cy, 0), 0.0)
        total += jnp.where(place < cells - cy, pltpu.roll(value, cells - cy, 0), 0.0)
        total += jnp.where(y_place > 0, pltpu.roll(value, 1, 0), 0.0)
        total += jnp.where(y_place < cy - 1, pltpu.roll(value, cells - 1, 0), 0.0)
        total += jnp.where(lane > 0, pltpu.roll(value, 1, 1), 0.0)
        total += jnp.where(lane < cx - 1, pltpu.roll(value, cx - 1, 1), 0.0)
        done[f] = value + diffusion_rates[f] * (total - 6.0 * value)

    spread_out[...] = jnp.transpose(jnp.where(same_x, 1.0, 0.0)).astype(jnp.bfloat16)
    tile_copy.wait()
    live_copy = pltpu.make_async_copy(live_hbm, live_ref, small_sem.at[0])
    live_copy.start()
    matrix_copy.wait()

    @pl.loop(0, rows * slots)
    def _(i):
        r, k = lax.div(i, slots), lax.rem(i, slots)
        flipped[r, k] = jnp.transpose(matrix[r, k].astype(jnp.float32)).astype(jnp.bfloat16)

    @pl.when(early)
    def _():
        pl.semaphore_wait(far_sem, n_all - n_first - late)
        each(lambda peer: ~first(peer), lambda peer: push(me * rows, rows, peer, 0))

    finish_faces(face_recv)

    shape = (32, 4 * cx)
    row, column = iota(shape, 0) & 15, iota(shape, 1)
    chosen = ((row < 8) & (column == (row >> 1) * cx) & ((row & 1) == 0)) | (
        (row >= 8) & (column == ((row - 8) >> 1) * cx + cx - 1) & ((row & 1) == 1)
    )
    sides = jnp.concatenate([x_in[0], x_in[1]], axis=0)
    upper = sides.astype(jnp.bfloat16).astype(jnp.float32)
    x_add = lax.dot_general(
        jnp.concatenate([upper, sides - upper], axis=0),
        jnp.where(chosen, 1.0, 0.0),
        TN,
        preferred_element_type=jnp.float32,
    )
    for f in (1, 2, 3, 0):
        rate = diffusion_rates[f]
        out = done.at[f]
        out[...] += rate * x_add[:, f * cx : (f + 1) * cx]
        out[pl.ds(0, cy), :] += rate * z_in[0, f]
        out[pl.ds(cells - cy, cy), :] += rate * z_in[1, f]
        out[pl.ds(0, cz, stride=cy), :] += rate * y_in[0, f]
        out[pl.ds(cy - 1, cz, stride=cy), :] += rate * y_in[1, f]

    live_copy.wait()
    settle(gathered.at[pl.ds(0, (n_all - 1) * rows)], recv_sem.at[0])

    for r in range(rows):
        for k in range(slots):
            tile = jnp.clip(tile_ref[r, k], 0, gathered.shape[0] - 1)
            picked_out[r, k] = jnp.where(k < live_ref[r], gathered[tile], 0.0)

    settle(gathered.at[pl.ds(0, (n_all - 1) * rows)], send_sem.at[0])
    finish_faces(face_send)


def finish(dims, swept, flipped, picked, box_mean, same_r, spread_x, *rest):
    outs, final, sem = rest[:5], rest[5], rest[6]
    cz, cy, cx = dims
    cells = cz * cy
    rows, slots, zone, _ = flipped.shape
    for i in (1, 2, 3):
        pltpu.make_async_copy(swept.at[i], outs[i], sem.at[0]).start()

    absorbed = []
    for r in range(rows):
        total = jnp.zeros((1, zone), jnp.float32)
        for k in range(slots):
            total += lax.dot_general(
                picked[r, k].astype(jnp.bfloat16),
                flipped[r, k],
                NN,
                preferred_element_type=jnp.float32,
            )
        absorbed.append(total)
    absorbed = jnp.concatenate(absorbed, axis=1)
    high = absorbed.astype(jnp.bfloat16).astype(jnp.float32)
    low = absorbed - high
    mask = same_r[...]
    both = jnp.concatenate([mask * high, mask * low], axis=0).astype(jnp.bfloat16)
    carried = lax.dot_general(both, spread_x[...], NN, preferred_element_type=jnp.float32)
    net = carried[: cells // BOX] + carried[cells // BOX :] - box_mean[...]
    source = jnp.broadcast_to(
        net.reshape(cz // BOX, 1, cy, cx), (cz // BOX, BOX, cy, cx)
    ).reshape(cells, cx)
    final[0] = source
    pltpu.make_async_copy(final.at[0], outs[4], sem.at[1]).start()
    final[1] = swept[0] + heating_rate * source
    pltpu.make_async_copy(final.at[1], outs[0], sem.at[1]).start()
    for ref, i in ((swept.at[pl.ds(1, 3)], 0), (final, 1)):
        pltpu.make_async_copy(ref, ref, sem.at[i]).wait()


def solution(mesh):
    counts = tuple(mesh.shape[a] for a in AXES)

    def local(kelvin, co2, h2o, soot, order, tiles, live, matrix):
        dims = kelvin.shape
        cz, cy, cx = dims
        cells = cz * cy
        rows = matrix.shape[0]
        zone = matrix.shape[2]
        blocks = counts[0] * counts[1] * counts[2] * rows
        flat = [a.reshape(cells, cx) for a in (kelvin, co2, h2o, soot)]
        order = order.reshape(1, -1)
        anywhere = pl.BlockSpec(memory_space=pl.ANY)
        f32 = jnp.float32
        vmem = pl.BlockSpec(memory_space=pltpu.VMEM)
        zones = order.shape[1]
        slots = matrix.shape[1]
        parts = pl.pallas_call(
            functools.partial(kernel, dims, counts),
            out_shape=[
                pltpu.VMEM((4, cells, cx), f32),
                pltpu.VMEM(matrix.shape, matrix.dtype),
                pltpu.VMEM((rows, slots, 1, zone), f32),
                pltpu.VMEM((cells // BOX, cx), f32),
                pltpu.VMEM((cells // BOX, zones), f32),
                pltpu.VMEM((zones, cx), jnp.bfloat16),
            ],
            in_specs=[anywhere] * 8,
            out_specs=[vmem] * 6,
            scratch_shapes=[
                pltpu.VMEM((4, cells, cx), f32),
                pltpu.VMEM(order.shape, jnp.int32),
                pltpu.VMEM(matrix.shape, matrix.dtype),
                pltpu.VMEM((blocks, 1, zone), f32),
                pltpu.VMEM((2, 4, cy, cx), f32),
                pltpu.VMEM((2, 4, cz, cx), f32),
                pltpu.VMEM((8, cells), f32),
                pltpu.VMEM((2, 4, cy, cx), f32),
                pltpu.VMEM((2, 4, cz, cx), f32),
                pltpu.VMEM((2, 8, cells), f32),
                pltpu.SMEM(tiles.shape, tiles.dtype),
                pltpu.SMEM(live.shape, live.dtype),
                pltpu.SemaphoreType.DMA((1,)),
                pltpu.SemaphoreType.DMA((1,)),
                pltpu.SemaphoreType.DMA((3,)),
                pltpu.SemaphoreType.DMA((3,)),
                pltpu.SemaphoreType.DMA((1,)),
                pltpu.SemaphoreType.DMA((1,)),
                pltpu.SemaphoreType.REGULAR,
            ],
            compiler_params=pltpu.CompilerParams(collective_id=0, has_side_effects=True),
        )(*flat, order, tiles, live, matrix)
        outs = pl.pallas_call(
            functools.partial(finish, dims),
            out_shape=[jax.ShapeDtypeStruct((cells, cx), f32)] * 5,
            in_specs=[vmem] * 6,
            out_specs=[anywhere] * 5,
            scratch_shapes=[
                pltpu.VMEM((2, cells, cx), f32),
                pltpu.SemaphoreType.DMA((2,)),
            ],
            compiler_params=pltpu.CompilerParams(vmem_limit_bytes=16 << 20),
        )(*parts)
        return tuple(o.reshape(dims) for o in outs)

    cell = P("blk", "gy", "sec")
    block = P(AXES)
    return jax.shard_map(
        local,
        mesh=mesh,
        in_specs=(cell,) * 4 + (P("sec", "blk", "gy", None), P(AXES, None), block, P(AXES, None, None, None)),
        out_specs=(cell,) * 5,
        check_vma=False,
    )
```

```python
import functools
import itertools

import jax
import jax.numpy as jnp
from jax import lax
from jax.experimental import pallas as pl
from jax.experimental.pallas import tpu as pltpu
from jax.sharding import PartitionSpec as P

BOX = 4
AXES = ("sec", "blk", "gy")

diffusion_rates = (0.12, 0.1, 0.1, 0.02)
vapour_attenuation_rate = (0.4, 1.6, 6.4, 25.6)
mixture_share_offset = (0.3, 0.25, 0.2, 0.15)
mixture_share_slope = (-0.05, 0.02, 0.03, 0.01)
particulate_attenuation_rate = 1.5
radiance_multiplier = 0.05
heating_rate = 0.1

SHARE_OFFSET = sum(mixture_share_offset)
SHARE_SLOPE = sum(mixture_share_slope)
VAPOUR_OFFSET = sum(b * k for b, k in zip(mixture_share_offset, vapour_attenuation_rate))
VAPOUR_SLOPE = sum(c * k for c, k in zip(mixture_share_slope, vapour_attenuation_rate))

MEAN = radiance_multiplier / BOX**3
MEAN_SOOT = MEAN * particulate_attenuation_rate

MESH = pl.DeviceIdType.MESH
NN = (((1,), (0,)), ((), ()))
NT = (((1,), (1,)), ((), ()))
TN = (((0,), (0,)), ((), ()))


def iota(shape, dim):
    return lax.broadcasted_iota(jnp.int32, shape, dim)


def group_sum(value, axis):
    size = value.shape[axis]
    place = iota(value.shape, axis)
    for step in (1, 2):
        above = pltpu.roll(value, size - step, axis)
        below = pltpu.roll(value, step, axis)
        value = value + jnp.where((place & step) == 0, above, below)
    return value


def kernel(
    dims,
    counts,
    kelvin_hbm,
    co2_hbm,
    h2o_hbm,
    soot_hbm,
    order_hbm,
    tile_hbm,
    live_hbm,
    matrix_hbm,
    *rest,
):
    done, flipped, own_out, picked_out, mean_out, rows_out, spread_out = rest[:7]
    (
        fields,
        order_ref,
        matrix,
        gathered,
        z_out,
        y_out,
        x_out,
        z_in,
        y_in,
        x_in,
        tile_ref,
        live_ref,
        field_sem,
        face_send,
        face_recv,
        send_sem,
        recv_sem,
        far_sem,
    ) = rest[7:]
    cz, cy, cx = dims
    n_sec, n_blk, n_gy = counts
    cells = cz * cy
    rows = matrix.shape[0]
    slots = matrix.shape[1]
    zones = order_ref.shape[1]
    zone = zones // rows
    n_plane = n_blk * n_gy
    sec, blk, gy = (lax.axis_index(a) for a in AXES)
    plane = blk * n_gy + gy
    me = sec * n_plane + plane
    n_all = n_sec * n_plane

    n_slab = cz // BOX
    slab = BOX * cy
    pltpu.make_async_copy(order_hbm, order_ref, send_sem.at[0]).start()
    for t in range(n_slab):
        part = pl.ds(t * slab, slab)
        for i, src in enumerate((kelvin_hbm, co2_hbm, h2o_hbm, soot_hbm)):
            pltpu.make_async_copy(src.at[part], fields.at[i, part], field_sem.at[0]).start()

    def settle(ref, sem):
        pltpu.make_async_copy(ref, ref, sem).wait()

    level = n_sec * n_blk

    def both(a, b):
        return jnp.logical_and(a, b)

    def either(a, b):
        return jnp.logical_or(a, b)

    def steps(sec, blk, gy):
        return sec // 2 + blk + gy

    def beside(peer):
        away = [abs(peer[a] - at) for a, at in zip(AXES, (sec, blk, gy))]
        return away[0] + away[1] + away[2] == 1

    def each(chosen, body):
        if n_all <= 32:
            for r in range(n_all):
                peer = {"sec": r % n_sec, "blk": r // n_sec % n_blk, "gy": r // level}

                @pl.when(chosen(peer))
                def _(peer=peer):
                    body(peer)
        else:

            @pl.loop(0, n_all)
            def _(r):
                peer = {
                    "sec": lax.rem(r, n_sec),
                    "blk": lax.rem(lax.div(r, n_sec), n_blk),
                    "gy": lax.div(r, level),
                }

                @pl.when(chosen(peer))
                def _():
                    body(peer)

    def other(peer):
        return (peer["sec"] * n_blk + peer["blk"]) * n_gy + peer["gy"] != me

    longest = (n_sec - 1) // 2 + n_blk + n_gy - 2

    def far(peer):
        return jnp.asarray(steps(**peer) > longest - 2)

    def middle(peer):
        return both(~far(peer), steps(**peer) > 0)

    me_at = dict(zip(AXES, (sec, blk, gy)))
    distant, early = far(me_at), middle(me_at)
    start, last = steps(**me_at) == 0, steps(**me_at) == longest
    n_far = sum(
        a // 2 + b + c > longest - 2
        for a in range(n_sec)
        for b in range(n_blk)
        for c in range(n_gy)
    )

    def greeted(peer):
        return both(other(peer), either(~distant, either(~middle(peer), beside(peer))))

    def greet(sem):
        return lambda peer: pl.semaphore_signal(
            sem, inc=1, device_id=peer, device_id_type=MESH
        )

    barrier = pltpu.get_barrier_semaphore()
    each(greeted, greet(barrier))

    places = (("sec", sec, n_sec), ("blk", blk, n_blk), ("gy", gy, n_gy))
    late = jnp.int32(0)
    for axis, at, size in places:
        for move, inside in ((-1, at > 0), (1, at < size - 1)):
            there = {**me_at, axis: at + move}
            late += both(inside, far(there)).astype(jnp.int32)

    def enter():
        pl.semaphore_wait(barrier, jnp.where(early, n_all - n_far - 1 + late, n_all - 1))
        each(
            lambda peer: both(middle(peer), both(distant, ~beside(peer))),
            greet(far_sem),
        )

    @pl.when(last)
    def _():
        enter()

    landing = (x_in, z_in, y_in)
    leaving = (x_out, z_out, y_out)
    for (_, at, size), land in zip(places, landing):
        for side, edge in ((0, 0), (1, size - 1)):

            @pl.when(at == edge)
            def _(land=land, side=side):
                land[side] = jnp.zeros(land.shape[1:], land.dtype)

    settle(order_ref, send_sem.at[0])
    order = order_ref[...]
    across = cx // BOX
    x_shape = (cx, zones)
    r_shape = (cells // BOX, zones)
    x_at = iota(x_shape, 0)
    r_at = iota(r_shape, 0)
    same_x = lax.rem(order, across) == lax.div(x_at, BOX)
    box_row = lax.div(r_at, cy) * (cy // BOX) + lax.div(lax.rem(r_at, cy), BOX)
    same_r = lax.div(order, across) == box_row
    spread_x = jnp.where(same_x, 1.0, 0.0).astype(jnp.bfloat16)
    rows_out[...] = jnp.where(same_r, 1.0, 0.0)
    total = jnp.zeros((cy, zones), jnp.float32)
    means = []
    settle(fields, field_sem.at[0])
    halves = []
    for t in range(n_slab):
        kelvin, co2, h2o, soot = (fields[i, pl.ds(t * slab, slab), :] for i in range(4))
        share = (co2 + h2o) * (MEAN * VAPOUR_OFFSET + MEAN * VAPOUR_SLOPE * kelvin) + (
            soot * kelvin
        ) * (MEAN_SOOT * SHARE_OFFSET + MEAN_SOOT * SHARE_SLOPE * kelvin)
        squared = kelvin * kelvin
        emission = (squared * squared) * share
        emission = emission.reshape(BOX, cy, cx)
        mean = emission[0] + emission[1] + emission[2] + emission[3]
        means.append(mean)
        upper = mean.astype(jnp.bfloat16).astype(jnp.float32)
        halves.append(jnp.concatenate([upper, mean - upper], axis=1))
    by_row = jnp.dot(
        jnp.concatenate(halves, axis=0).astype(jnp.bfloat16),
        jnp.concatenate([spread_x, spread_x], axis=0),
        preferred_element_type=jnp.float32,
    )
    for t in range(n_slab):
        part = slice(t * cy, (t + 1) * cy)
        total += jnp.where(same_r[part], by_row[part], 0.0)
    slabs = jnp.concatenate(means, axis=0)
    emitted = jnp.sum(total, axis=0, keepdims=True)
    for r in range(rows):
        gathered[me * rows + r] = emitted[:, r * zone : (r + 1) * zone]
    matrix_copy = pltpu.make_async_copy(matrix_hbm, matrix, field_sem.at[0])
    matrix_copy.start()

    def push(start, length, peer, stage):
        block = gathered.at[pl.ds(start, length)]
        pltpu.make_async_remote_copy(
            src_ref=block,
            dst_ref=block,
            send_sem=send_sem.at[stage],
            recv_sem=recv_sem.at[stage],
            device_id=peer,
            device_id_type=MESH,
        ).start()

    lane = iota((cells, cx), 1)

    def idle():
        mean_out[...] = group_sum(group_sum(slabs, 0), 1)
        place = iota((cells, cx), 0)
        y_place = lax.rem(place, cy)
        for f in range(4):
            value = fields[f]
            total = jnp.where(place >= cy, pltpu.roll(value, cy, 0), 0.0)
            total += jnp.where(place < cells - cy, pltpu.roll(value, cells - cy, 0), 0.0)
            total += jnp.where(y_place > 0, pltpu.roll(value, 1, 0), 0.0)
            total += jnp.where(y_place < cy - 1, pltpu.roll(value, cells - 1, 0), 0.0)
            total += jnp.where(lane > 0, pltpu.roll(value, 1, 1), 0.0)
            total += jnp.where(lane < cx - 1, pltpu.roll(value, cx - 1, 1), 0.0)
            done[f] = value + diffusion_rates[f] * (total - 6.0 * value)

        spread_out[...] = jnp.transpose(jnp.where(same_x, 1.0, 0.0)).astype(jnp.bfloat16)
        matrix_copy.wait()
        tile_copy = pltpu.make_async_copy(tile_hbm, tile_ref, field_sem.at[0])
        tile_copy.start()

        for r in range(rows):
            own_out[r] = lax.dot_general(
                gathered[me * rows + r].astype(jnp.bfloat16),
                matrix[r, 0],
                NT,
                preferred_element_type=jnp.float32,
            )

        @pl.loop(0, rows * (slots - 1))
        def _(i):
            r, k = lax.div(i, slots - 1), lax.rem(i, slots - 1)
            flipped[r, k] = jnp.transpose(matrix[r, k + 1].astype(jnp.float32)).astype(jnp.bfloat16)

        tile_copy.wait()
        live_copy = pltpu.make_async_copy(live_hbm, live_ref, field_sem.at[0])
        live_copy.start()
        live_copy.wait()

    @pl.when(start)
    def _():
        idle()

    @pl.when(~last)
    def _():
        enter()

    each(
        lambda peer: both(other(peer), either(~early, ~far(peer))),
        lambda peer: push(me * rows, rows, peer, 0),
    )

    packed = jnp.zeros((cells, cx), jnp.float32)
    for f in range(4):
        field = fields.at[f]
        z_out[0, f] = field[pl.ds(0, cy), :]
        z_out[1, f] = field[pl.ds(cells - cy, cy), :]
        y_out[0, f] = field[pl.ds(0, cz, stride=cy), :]
        y_out[1, f] = field[pl.ds(cy - 1, cz, stride=cy), :]
        packed = jnp.where((lane >> 1) == f, pltpu.roll(field[...], 2 * f + 1, 1), packed)
    x_out[...] = jnp.transpose(packed)[:8]

    def face(which, side):
        axis, at, _ = places[which]
        source = x_out if which == 0 else leaving[which].at[side]
        return pltpu.make_async_remote_copy(
            src_ref=source,
            dst_ref=landing[which].at[1 - side],
            send_sem=face_send.at[0],
            recv_sem=face_recv.at[0],
            device_id={axis: at + (2 * side - 1)},
            device_id_type=MESH,
        )

    def has(which, side):
        _, at, size = places[which]
        return at > 0 if side == 0 else at < size - 1

    def finish_faces(sem):
        options = [(min(size - 1, 1), 2)[: min(size - 1, 2) or 1] for _, _, size in places]
        sides = [
            has(which, 0).astype(jnp.int32) + has(which, 1).astype(jnp.int32) for which in range(3)
        ]
        lines = (8 * cells // cx, 4 * cy, 4 * cz)
        for counts in itertools.product(*options):
            met = functools.reduce(both, [side == count for side, count in zip(sides, counts)])
            total = sum(line * count for line, count in zip(lines, counts))

            @pl.when(met)
            def _(total=total):
                settle(fields.at[pl.ds(0, 2), pl.ds(0, total // 2)], sem.at[0])

    def launch(side):
        for which in (1, 2, 0):

            @pl.when(has(which, side))
            def _(which=which):
                face(which, side).start()

    launch(0)
    launch(1)

    @pl.when(~start)
    def _():
        idle()

    @pl.when(early)
    def _():
        pl.semaphore_wait(far_sem, n_far - late)
        each(far, lambda peer: push(me * rows, rows, peer, 0))

    finish_faces(face_recv)

    shape = (32, 4 * cx)
    row, column = iota(shape, 0) & 15, iota(shape, 1)
    chosen = ((row < 8) & (column == (row >> 1) * cx) & ((row & 1) == 0)) | (
        (row >= 8) & (column == ((row - 8) >> 1) * cx + cx - 1) & ((row & 1) == 1)
    )
    sides = jnp.concatenate([x_in[0], x_in[1]], axis=0)
    upper = sides.astype(jnp.bfloat16).astype(jnp.float32)
    x_add = lax.dot_general(
        jnp.concatenate([upper, sides - upper], axis=0),
        jnp.where(chosen, 1.0, 0.0),
        TN,
        preferred_element_type=jnp.float32,
    )
    for f in (1, 2, 3, 0):
        rate = diffusion_rates[f]
        out = done.at[f]
        out[...] += rate * x_add[:, f * cx : (f + 1) * cx]
        out[pl.ds(0, cy), :] += rate * z_in[0, f]
        out[pl.ds(cells - cy, cy), :] += rate * z_in[1, f]
        out[pl.ds(0, cz, stride=cy), :] += rate * y_in[0, f]
        out[pl.ds(cy - 1, cz, stride=cy), :] += rate * y_in[1, f]

    settle(gathered.at[pl.ds(0, (n_all - 1) * rows)], recv_sem.at[0])

    for r in range(rows):
        for k in range(1, slots):
            tile = jnp.clip(tile_ref[r, k], 0, gathered.shape[0] - 1)
            picked_out[r, k - 1] = jnp.where(k < live_ref[r], gathered[tile], 0.0)

    settle(gathered.at[pl.ds(0, (n_all - 1) * rows)], send_sem.at[0])
    finish_faces(face_send)


def finish(dims, swept, flipped, own, picked, box_mean, same_r, spread_x, *rest):
    outs, final, sem = rest[:5], rest[5], rest[6]
    cz, cy, cx = dims
    cells = cz * cy
    rows, slots, zone, _ = flipped.shape
    @pl.when(lax.axis_index("sec") >= 0)
    def _():
        for i in (1, 2, 3):
            pltpu.make_async_copy(swept.at[i], outs[i], sem.at[0]).start()

    absorbed = []
    for r in range(rows):
        total = own[r]
        for k in range(slots):
            total += lax.dot_general(
                picked[r, k].astype(jnp.bfloat16),
                flipped[r, k],
                NN,
                preferred_element_type=jnp.float32,
            )
        absorbed.append(total)
    absorbed = jnp.concatenate(absorbed, axis=1)
    high = absorbed.astype(jnp.bfloat16).astype(jnp.float32)
    low = absorbed - high
    mask = same_r[...]
    both = jnp.concatenate([mask * high, mask * low], axis=0).astype(jnp.bfloat16)
    carried = lax.dot_general(both, spread_x[...], NN, preferred_element_type=jnp.float32)
    net = carried[: cells // BOX] + carried[cells // BOX :] - box_mean[...]
    slab = BOX * cy
    for t in range(cz // BOX):
        part = pl.ds(t * slab, slab)
        piece = jnp.broadcast_to(net[None, t * cy : (t + 1) * cy], (BOX, cy, cx)).reshape(slab, cx)
        final[0, part] = piece
        final[1, part] = swept[0, part] + heating_rate * piece
        for i, out in enumerate((outs[4], outs[0])):
            pltpu.make_async_copy(final.at[i, part], out.at[part], sem.at[1]).start()
    for ref, i in ((swept.at[pl.ds(1, 3)], 0), (final, 1)):
        pltpu.make_async_copy(ref, ref, sem.at[i]).wait()


def solution(mesh):
    counts = tuple(mesh.shape[a] for a in AXES)

    def local(kelvin, co2, h2o, soot, order, tiles, live, matrix):
        dims = kelvin.shape
        cz, cy, cx = dims
        cells = cz * cy
        rows = matrix.shape[0]
        zone = matrix.shape[2]
        blocks = counts[0] * counts[1] * counts[2] * rows
        flat = [a.reshape(cells, cx) for a in (kelvin, co2, h2o, soot)]
        order = order.reshape(1, -1)
        anywhere = pl.BlockSpec(memory_space=pl.ANY)
        f32 = jnp.float32
        vmem = pl.BlockSpec(memory_space=pltpu.VMEM)
        zones = order.shape[1]
        slots = matrix.shape[1]
        parts = pl.pallas_call(
            functools.partial(kernel, dims, counts),
            out_shape=[
                pltpu.VMEM((4, cells, cx), f32),
                pltpu.VMEM((rows, slots - 1, zone, zone), matrix.dtype),
                pltpu.VMEM((rows, 1, zone), f32),
                pltpu.VMEM((rows, slots - 1, 1, zone), f32),
                pltpu.VMEM((cells // BOX, cx), f32),
                pltpu.VMEM((cells // BOX, zones), f32),
                pltpu.VMEM((zones, cx), jnp.bfloat16),
            ],
            in_specs=[anywhere] * 8,
            out_specs=[vmem] * 7,
            scratch_shapes=[
                pltpu.VMEM((4, cells, cx), f32),
                pltpu.VMEM(order.shape, jnp.int32),
                pltpu.VMEM(matrix.shape, matrix.dtype),
                pltpu.VMEM((blocks, 1, zone), f32),
                pltpu.VMEM((2, 4, cy, cx), f32),
                pltpu.VMEM((2, 4, cz, cx), f32),
                pltpu.VMEM((8, cells), f32),
                pltpu.VMEM((2, 4, cy, cx), f32),
                pltpu.VMEM((2, 4, cz, cx), f32),
                pltpu.VMEM((2, 8, cells), f32),
                pltpu.SMEM(tiles.shape, tiles.dtype),
                pltpu.SMEM(live.shape, live.dtype),
                pltpu.SemaphoreType.DMA((1,)),
                pltpu.SemaphoreType.DMA((1,)),
                pltpu.SemaphoreType.DMA((1,)),
                pltpu.SemaphoreType.DMA((1,)),
                pltpu.SemaphoreType.DMA((1,)),
                pltpu.SemaphoreType.REGULAR,
            ],
            compiler_params=pltpu.CompilerParams(collective_id=0, has_side_effects=True),
        )(*flat, order, tiles, live, matrix)
        outs = pl.pallas_call(
            functools.partial(finish, dims),
            out_shape=[jax.ShapeDtypeStruct((cells, cx), f32)] * 5,
            in_specs=[vmem] * 7,
            out_specs=[anywhere] * 5,
            scratch_shapes=[
                pltpu.VMEM((2, cells, cx), f32),
                pltpu.SemaphoreType.DMA((2,)),
            ],
            compiler_params=pltpu.CompilerParams(vmem_limit_bytes=16 << 20),
        )(*parts)
        return tuple(o.reshape(dims) for o in outs)

    cell = P("blk", "gy", "sec")
    block = P(AXES)
    return jax.shard_map(
        local,
        mesh=mesh,
        in_specs=(cell,) * 4 + (P("sec", "blk", "gy", None), P(AXES, None), block, P(AXES, None, None, None)),
        out_specs=(cell,) * 5,
        check_vma=False,
    )
```

```python
import functools
import itertools

import jax
import jax.numpy as jnp
from jax import lax
from jax.experimental import pallas as pl
from jax.experimental.pallas import tpu as pltpu
from jax.sharding import PartitionSpec as P

BOX = 4
AXES = ("sec", "blk", "gy")

diffusion_rates = (0.12, 0.1, 0.1, 0.02)
vapour_attenuation_rate = (0.4, 1.6, 6.4, 25.6)
mixture_share_offset = (0.3, 0.25, 0.2, 0.15)
mixture_share_slope = (-0.05, 0.02, 0.03, 0.01)
particulate_attenuation_rate = 1.5
radiance_multiplier = 0.05
heating_rate = 0.1

SHARE_OFFSET = sum(mixture_share_offset)
SHARE_SLOPE = sum(mixture_share_slope)
VAPOUR_OFFSET = sum(b * k for b, k in zip(mixture_share_offset, vapour_attenuation_rate))
VAPOUR_SLOPE = sum(c * k for c, k in zip(mixture_share_slope, vapour_attenuation_rate))

MEAN = radiance_multiplier / BOX**3
MEAN_SOOT = MEAN * particulate_attenuation_rate

MESH = pl.DeviceIdType.MESH
NN = (((1,), (0,)), ((), ()))
NT = (((1,), (1,)), ((), ()))
TN = (((0,), (0,)), ((), ()))


def iota(shape, dim):
    return lax.broadcasted_iota(jnp.int32, shape, dim)


def group_sum(value, axis):
    size = value.shape[axis]
    place = iota(value.shape, axis)
    for step in (1, 2):
        above = pltpu.roll(value, size - step, axis)
        below = pltpu.roll(value, step, axis)
        value = value + jnp.where((place & step) == 0, above, below)
    return value


def kernel(
    dims,
    counts,
    kelvin_hbm,
    co2_hbm,
    h2o_hbm,
    soot_hbm,
    order_hbm,
    tile_hbm,
    live_hbm,
    matrix_hbm,
    *rest,
):
    done, flipped, own_out, picked_out, mean_out, rows_out, spread_out = rest[:7]
    (
        fields,
        order_ref,
        matrix,
        gathered,
        z_out,
        y_out,
        x_out,
        z_in,
        y_in,
        x_in,
        tile_ref,
        live_ref,
        field_sem,
        amount,
        face_recv,
        send_sem,
        recv_sem,
        far_sem,
    ) = rest[7:]
    cz, cy, cx = dims
    n_sec, n_blk, n_gy = counts
    cells = cz * cy
    rows = matrix.shape[0]
    slots = matrix.shape[1]
    zones = order_ref.shape[1]
    zone = zones // rows
    n_plane = n_blk * n_gy
    sec, blk, gy = (lax.axis_index(a) for a in AXES)
    plane = blk * n_gy + gy
    me = sec * n_plane + plane
    n_all = n_sec * n_plane

    n_slab = cz // BOX
    slab = BOX * cy
    pltpu.make_async_copy(order_hbm, order_ref, send_sem.at[0]).start()
    for t in range(n_slab):
        part = pl.ds(t * slab, slab)
        for i, src in enumerate((kelvin_hbm, co2_hbm, h2o_hbm, soot_hbm)):
            pltpu.make_async_copy(src.at[part], fields.at[i, part], field_sem.at[0]).start()

    def settle(ref, sem):
        pltpu.make_async_copy(ref, ref, sem).wait()

    level = n_sec * n_blk

    def both(a, b):
        return jnp.logical_and(a, b)

    def either(a, b):
        return jnp.logical_or(a, b)

    def steps(sec, blk, gy):
        return sec // 2 + blk + gy

    def beside(peer):
        away = [abs(peer[a] - at) for a, at in zip(AXES, (sec, blk, gy))]
        return away[0] + away[1] + away[2] == 1

    def each(chosen, body):
        if n_all <= 32:
            for r in range(n_all):
                peer = {"sec": r % n_sec, "blk": r // n_sec % n_blk, "gy": r // level}

                @pl.when(chosen(peer))
                def _(peer=peer):
                    body(peer)
        else:

            @pl.loop(0, n_all)
            def _(r):
                peer = {
                    "sec": lax.rem(r, n_sec),
                    "blk": lax.rem(lax.div(r, n_sec), n_blk),
                    "gy": lax.div(r, level),
                }

                @pl.when(chosen(peer))
                def _():
                    body(peer)

    def other(peer):
        return (peer["sec"] * n_blk + peer["blk"]) * n_gy + peer["gy"] != me

    longest = (n_sec - 1) // 2 + n_blk + n_gy - 2

    def far(peer):
        return jnp.asarray(steps(**peer) > longest - 2)

    def middle(peer):
        return both(~far(peer), steps(**peer) > 0)

    me_at = dict(zip(AXES, (sec, blk, gy)))
    distant, early = far(me_at), middle(me_at)
    start = steps(**me_at) == 0
    n_far = sum(
        a // 2 + b + c > longest - 2
        for a in range(n_sec)
        for b in range(n_blk)
        for c in range(n_gy)
    )

    def greeted(peer):
        return both(other(peer), either(~distant, either(~middle(peer), beside(peer))))

    def greet(sem):
        return lambda peer: pl.semaphore_signal(
            sem, inc=1, device_id=peer, device_id_type=MESH
        )

    barrier = pltpu.get_barrier_semaphore()
    each(greeted, greet(barrier))

    places = (("sec", sec, n_sec), ("blk", blk, n_blk), ("gy", gy, n_gy))
    late = jnp.int32(0)
    for axis, at, size in places:
        for move, inside in ((-1, at > 0), (1, at < size - 1)):
            there = {**me_at, axis: at + move}
            late += both(inside, far(there)).astype(jnp.int32)

    landing = (x_in, z_in, y_in)
    leaving = (x_out, z_out, y_out)
    for (_, at, size), land in zip(places, landing):
        for side, edge in ((0, 0), (1, size - 1)):

            @pl.when(at == edge)
            def _(land=land, side=side):
                land[side] = jnp.zeros(land.shape[1:], land.dtype)

    settle(order_ref, send_sem.at[0])
    order = order_ref[...]
    across = cx // BOX
    x_shape = (cx, zones)
    r_shape = (cells // BOX, zones)
    x_at = iota(x_shape, 0)
    r_at = iota(r_shape, 0)
    same_x = lax.rem(order, across) == lax.div(x_at, BOX)
    box_row = lax.div(r_at, cy) * (cy // BOX) + lax.div(lax.rem(r_at, cy), BOX)
    same_r = lax.div(order, across) == box_row
    spread_x = jnp.where(same_x, 1.0, 0.0).astype(jnp.bfloat16)
    rows_out[...] = jnp.where(same_r, 1.0, 0.0)
    total = jnp.zeros((cy, zones), jnp.float32)
    means = []
    settle(fields, field_sem.at[0])
    halves = []
    for t in range(n_slab):
        kelvin, co2, h2o, soot = (fields[i, pl.ds(t * slab, slab), :] for i in range(4))
        share = (co2 + h2o) * (MEAN * VAPOUR_OFFSET + MEAN * VAPOUR_SLOPE * kelvin) + (
            soot * kelvin
        ) * (MEAN_SOOT * SHARE_OFFSET + MEAN_SOOT * SHARE_SLOPE * kelvin)
        squared = kelvin * kelvin
        emission = (squared * squared) * share
        emission = emission.reshape(BOX, cy, cx)
        mean = emission[0] + emission[1] + emission[2] + emission[3]
        means.append(mean)
        upper = mean.astype(jnp.bfloat16).astype(jnp.float32)
        halves.append(jnp.concatenate([upper, mean - upper], axis=1))
    by_row = jnp.dot(
        jnp.concatenate(halves, axis=0).astype(jnp.bfloat16),
        jnp.concatenate([spread_x, spread_x], axis=0),
        preferred_element_type=jnp.float32,
    )
    for t in range(n_slab):
        part = slice(t * cy, (t + 1) * cy)
        total += jnp.where(same_r[part], by_row[part], 0.0)
    slabs = jnp.concatenate(means, axis=0)
    emitted = jnp.sum(total, axis=0, keepdims=True)
    for r in range(rows):
        gathered[me * rows + r] = emitted[:, r * zone : (r + 1) * zone]
    matrix_copy = pltpu.make_async_copy(matrix_hbm, matrix, field_sem.at[0])
    matrix_copy.start()

    def push(start, length, peer, stage):
        block = gathered.at[pl.ds(start, length)]
        pltpu.make_async_remote_copy(
            src_ref=block,
            dst_ref=block,
            send_sem=send_sem.at[stage],
            recv_sem=recv_sem.at[stage],
            device_id=peer,
            device_id_type=MESH,
        ).start()

    lane = iota((cells, cx), 1)

    def idle():
        mean_out[...] = group_sum(group_sum(slabs, 0), 1)
        place = iota((cells, cx), 0)
        y_place = lax.rem(place, cy)
        for f in range(4):
            value = fields[f]
            total = jnp.where(place >= cy, pltpu.roll(value, cy, 0), 0.0)
            total += jnp.where(place < cells - cy, pltpu.roll(value, cells - cy, 0), 0.0)
            total += jnp.where(y_place > 0, pltpu.roll(value, 1, 0), 0.0)
            total += jnp.where(y_place < cy - 1, pltpu.roll(value, cells - 1, 0), 0.0)
            total += jnp.where(lane > 0, pltpu.roll(value, 1, 1), 0.0)
            total += jnp.where(lane < cx - 1, pltpu.roll(value, cx - 1, 1), 0.0)
            done[f] = value + diffusion_rates[f] * (total - 6.0 * value)

        spread_out[...] = jnp.transpose(jnp.where(same_x, 1.0, 0.0)).astype(jnp.bfloat16)
        matrix_copy.wait()
        tile_copy = pltpu.make_async_copy(tile_hbm, tile_ref, field_sem.at[0])
        tile_copy.start()

        for r in range(rows):
            own_out[r] = lax.dot_general(
                gathered[me * rows + r].astype(jnp.bfloat16),
                matrix[r, 0],
                NT,
                preferred_element_type=jnp.float32,
            )

        @pl.loop(0, rows * (slots - 1))
        def _(i):
            r, k = lax.div(i, slots - 1), lax.rem(i, slots - 1)
            flipped[r, k] = jnp.transpose(matrix[r, k + 1].astype(jnp.float32)).astype(jnp.bfloat16)

        tile_copy.wait()
        live_copy = pltpu.make_async_copy(live_hbm, live_ref, field_sem.at[0])
        live_copy.start()
        live_copy.wait()

    @pl.when(start)
    def _():
        idle()

    pl.semaphore_wait(barrier, jnp.where(early, n_all - n_far - 1 + late, n_all - 1))

    each(
        lambda peer: both(other(peer), either(~early, ~far(peer))),
        lambda peer: push(me * rows, rows, peer, 0),
    )
    each(
        lambda peer: both(middle(peer), both(distant, ~beside(peer))),
        greet(far_sem),
    )

    packed = jnp.zeros((cells, cx), jnp.float32)
    for f in range(4):
        field = fields.at[f]
        z_out[0, f] = field[pl.ds(0, cy), :]
        z_out[1, f] = field[pl.ds(cells - cy, cy), :]
        y_out[0, f] = field[pl.ds(0, cz, stride=cy), :]
        y_out[1, f] = field[pl.ds(cy - 1, cz, stride=cy), :]
        packed = jnp.where((lane >> 1) == f, pltpu.roll(field[...], 2 * f + 1, 1), packed)
    x_out[...] = jnp.transpose(packed)[:8]

    def face(which, side):
        axis, at, _ = places[which]
        source = x_out if which == 0 else leaving[which].at[side]
        return pltpu.make_async_remote_copy(
            src_ref=source,
            dst_ref=landing[which].at[1 - side],
            send_sem=send_sem.at[0],
            recv_sem=face_recv.at[0],
            device_id={axis: at + (2 * side - 1)},
            device_id_type=MESH,
        )

    def has(which, side):
        _, at, size = places[which]
        return at > 0 if side == 0 else at < size - 1

    def finish_faces(sem, more):
        options = [(min(size - 1, 1), 2)[: min(size - 1, 2) or 1] for _, _, size in places]
        sides = [
            has(which, 0).astype(jnp.int32) + has(which, 1).astype(jnp.int32) for which in range(3)
        ]
        lines = (8 * cells // cx, 4 * cy, 4 * cz)
        for counts in itertools.product(*options):
            met = functools.reduce(both, [side == count for side, count in zip(sides, counts)])
            total = more + sum(line * count for line, count in zip(lines, counts))

            @pl.when(met)
            def _(total=total):
                settle(amount.at[pl.ds(0, total)], sem.at[0])

    def launch(side):
        for which in (1, 2, 0):

            @pl.when(has(which, side))
            def _(which=which):
                face(which, side).start()

    launch(0)
    launch(1)

    @pl.when(~start)
    def _():
        idle()

    @pl.when(early)
    def _():
        pl.semaphore_wait(far_sem, n_far - late)
        each(far, lambda peer: push(me * rows, rows, peer, 0))

    finish_faces(face_recv, 0)

    shape = (32, 4 * cx)
    row, column = iota(shape, 0) & 15, iota(shape, 1)
    chosen = ((row < 8) & (column == (row >> 1) * cx) & ((row & 1) == 0)) | (
        (row >= 8) & (column == ((row - 8) >> 1) * cx + cx - 1) & ((row & 1) == 1)
    )
    sides = jnp.concatenate([x_in[0], x_in[1]], axis=0)
    upper = sides.astype(jnp.bfloat16).astype(jnp.float32)
    x_add = lax.dot_general(
        jnp.concatenate([upper, sides - upper], axis=0),
        jnp.where(chosen, 1.0, 0.0),
        TN,
        preferred_element_type=jnp.float32,
    )
    for f in (1, 2, 3, 0):
        rate = diffusion_rates[f]
        out = done.at[f]
        out[...] += rate * x_add[:, f * cx : (f + 1) * cx]
        out[pl.ds(0, cy), :] += rate * z_in[0, f]
        out[pl.ds(cells - cy, cy), :] += rate * z_in[1, f]
        out[pl.ds(0, cz, stride=cy), :] += rate * y_in[0, f]
        out[pl.ds(cy - 1, cz, stride=cy), :] += rate * y_in[1, f]

    settle(gathered.at[pl.ds(0, (n_all - 1) * rows)], recv_sem.at[0])

    for r in range(rows):
        for k in range(1, slots):
            tile = jnp.clip(tile_ref[r, k], 0, gathered.shape[0] - 1)
            picked_out[r, k - 1] = jnp.where(k < live_ref[r], gathered[tile], 0.0)

    finish_faces(send_sem, (n_all - 1) * zones // cx)


def finish(dims, swept, flipped, own, picked, box_mean, same_r, spread_x, *rest):
    outs, final, sem = rest[:5], rest[5], rest[6]
    cz, cy, cx = dims
    cells = cz * cy
    rows, slots, zone, _ = flipped.shape
    @pl.when(lax.axis_index("sec") >= 0)
    def _():
        for i in (1, 2, 3):
            pltpu.make_async_copy(swept.at[i], outs[i], sem.at[0]).start()

    absorbed = []
    for r in range(rows):
        total = own[r]
        for k in range(slots):
            total += lax.dot_general(
                picked[r, k].astype(jnp.bfloat16),
                flipped[r, k],
                NN,
                preferred_element_type=jnp.float32,
            )
        absorbed.append(total)
    absorbed = jnp.concatenate(absorbed, axis=1)
    high = absorbed.astype(jnp.bfloat16).astype(jnp.float32)
    low = absorbed - high
    mask = same_r[...]
    both = jnp.concatenate([mask * high, mask * low], axis=0).astype(jnp.bfloat16)
    carried = lax.dot_general(both, spread_x[...], NN, preferred_element_type=jnp.float32)
    net = carried[: cells // BOX] + carried[cells // BOX :] - box_mean[...]
    slab = BOX * cy
    for t in range(cz // BOX):
        part = pl.ds(t * slab, slab)
        piece = jnp.broadcast_to(net[None, t * cy : (t + 1) * cy], (BOX, cy, cx)).reshape(slab, cx)
        final[0, part] = piece
        final[1, part] = swept[0, part] + heating_rate * piece
        for i, out in enumerate((outs[4], outs[0])):
            pltpu.make_async_copy(final.at[i, part], out.at[part], sem.at[0]).start()
    pltpu.make_async_copy(final, final, sem.at[0]).wait()


def solution(mesh):
    counts = tuple(mesh.shape[a] for a in AXES)

    def local(kelvin, co2, h2o, soot, order, tiles, live, matrix):
        dims = kelvin.shape
        cz, cy, cx = dims
        cells = cz * cy
        rows = matrix.shape[0]
        zone = matrix.shape[2]
        n_devices = counts[0] * counts[1] * counts[2]
        blocks = n_devices * rows
        flat = [a.reshape(cells, cx) for a in (kelvin, co2, h2o, soot)]
        order = order.reshape(1, -1)
        anywhere = pl.BlockSpec(memory_space=pl.ANY)
        f32 = jnp.float32
        vmem = pl.BlockSpec(memory_space=pltpu.VMEM)
        zones = order.shape[1]
        slots = matrix.shape[1]
        most = (n_devices - 1) * zones // cx + 2 * (8 * cells // cx + 4 * cy + 4 * cz)
        parts = pl.pallas_call(
            functools.partial(kernel, dims, counts),
            out_shape=[
                pltpu.VMEM((4, cells, cx), f32),
                pltpu.VMEM((rows, slots - 1, zone, zone), matrix.dtype),
                pltpu.VMEM((rows, 1, zone), f32),
                pltpu.VMEM((rows, slots - 1, 1, zone), f32),
                pltpu.VMEM((cells // BOX, cx), f32),
                pltpu.VMEM((cells // BOX, zones), f32),
                pltpu.VMEM((zones, cx), jnp.bfloat16),
            ],
            in_specs=[anywhere] * 8,
            out_specs=[vmem] * 7,
            scratch_shapes=[
                pltpu.VMEM((4, cells, cx), f32),
                pltpu.VMEM(order.shape, jnp.int32),
                pltpu.VMEM(matrix.shape, matrix.dtype),
                pltpu.VMEM((blocks, 1, zone), f32),
                pltpu.VMEM((2, 4, cy, cx), f32),
                pltpu.VMEM((2, 4, cz, cx), f32),
                pltpu.VMEM((8, cells), f32),
                pltpu.VMEM((2, 4, cy, cx), f32),
                pltpu.VMEM((2, 4, cz, cx), f32),
                pltpu.VMEM((2, 8, cells), f32),
                pltpu.SMEM(tiles.shape, tiles.dtype),
                pltpu.SMEM(live.shape, live.dtype),
                pltpu.SemaphoreType.DMA((1,)),
                pltpu.VMEM((most, 1, cx), f32),
                pltpu.SemaphoreType.DMA((1,)),
                pltpu.SemaphoreType.DMA((1,)),
                pltpu.SemaphoreType.DMA((1,)),
                pltpu.SemaphoreType.REGULAR,
            ],
            compiler_params=pltpu.CompilerParams(collective_id=0, has_side_effects=True),
        )(*flat, order, tiles, live, matrix)
        outs = pl.pallas_call(
            functools.partial(finish, dims),
            out_shape=[jax.ShapeDtypeStruct((cells, cx), f32)] * 5,
            in_specs=[vmem] * 7,
            out_specs=[anywhere] * 5,
            scratch_shapes=[
                pltpu.VMEM((5, cells, cx), f32),
                pltpu.SemaphoreType.DMA((1,)),
            ],
            compiler_params=pltpu.CompilerParams(vmem_limit_bytes=16 << 20),
        )(*parts)
        return tuple(o.reshape(dims) for o in outs)

    cell = P("blk", "gy", "sec")
    block = P(AXES)
    return jax.shard_map(
        local,
        mesh=mesh,
        in_specs=(cell,) * 4 + (P("sec", "blk", "gy", None), P(AXES, None), block, P(AXES, None, None, None)),
        out_specs=(cell,) * 5,
        check_vma=False,
    )
```
